256 devices in a mesh: lat: 32 (over y, z_lo, x), lon: 8 (over z_hi, core).
Axes of the slice: x: 4, y: 4, z: 8 (z_hi: 4, z_lo: 2; z = z_hi * 2 + z_lo), core: 2. Of those that a mesh axis runs over, the one named last changes fastest.
Arguments:
- tracers: float32 [2, 32, 512, 2048], P(None, None, 'lat', 'lon'), may hold values from -12 to 12
- east_velocity: bfloat16 [32, 512, 2048], P(None, 'lat', 'lon'), may hold values from -6 to 6
- north_velocity: bfloat16 [32, 512, 2048], P(None, 'lat', 'lon'), may hold values from -6 to 6
- column_levels: int32 [512, 2048], P('lat', 'lon'), may hold values from 0 to 32
- surface_term: float32 [512, 2048], P('lat', 'lon'), may hold values from 0.05 to 2
Outputs:
- updated: float32 [2, 32, 512, 2048], P(None, None, 'lat', 'lon')
- gradient: float32 [2, 512, 2048], P(None, 'lat', 'lon')
The draws below stay inside these ranges and needn't reach their ends.
Inputs may be any that keep to these rules, and one draw needn't show every extreme that they name: column_levels counts the ocean levels of a column; 0 is land.
All inputs are finite; a program needn't handle non-finite values.
Results may differ from the reference program's by a relative error of at most 0.0003.
Values may be sent and summed in bfloat16 or wider, within the bound.
A program may use at most 128 MiB of HBM per device.

```python
import math
import jax
import jax.numpy as jnp
from jax import lax

KZ = 32
ITERS = 4
NLAT = 512
NLON = 2048


def draw_tracers(key, part):
    key = jax.random.fold_in(key, 11)
    rough_key = jax.random.fold_in(key, 0)
    shape = (2, KZ, NLAT, NLON)
    position = jnp.arange(NLAT, dtype=jnp.float32) / NLAT
    rough = jnp.clip(jax.random.normal(rough_key, shape, jnp.float32), -6.0, 6.0)
    offset = 0.4 + 3.6 * position
    upper = (jnp.arange(KZ) < 4).astype(jnp.float32)
    which = jnp.array([1.0, 0.0], jnp.float32)
    field = rough + which[:, None, None, None] * upper[None, :, None, None] * offset[None, None, :, None]
    return field.astype(jnp.float32)


def place_ends(result, rng, smallest, top_value):
    longest = result.shape.index(max(result.shape))
    spots = []
    for shift in (0, 1):
        where = [jax.random.randint(jax.random.fold_in(rng, axis), (), 0, length) for axis, length in enumerate(result.shape)]
        where[longest] = (where[longest] + shift) % result.shape[longest]
        spots.append(tuple(where))
    return result.at[spots[0]].set(smallest).at[spots[1]].set(top_value)


def level_of(own_key, extent, cuts, least, high):
    gain, own = 1.0, jax.random.fold_in(own_key, 6)
    for dim, blocks in cuts:
        steps = jnp.exp(jax.random.uniform(jax.random.fold_in(own, dim), (blocks,), jnp.float32, least / len(cuts), high / len(cuts)))
        gain = gain * jnp.repeat(steps, extent[dim] // blocks).reshape([-1 if axis == dim else 1 for axis in range(len(extent))])
    return gain


def scatter_about(key, dims, scale, limit, cuts=(), kind=jnp.bfloat16):
    values = jax.random.normal(key, dims, jnp.float32) * scale
    if len(cuts) > 0:
        values = level_of(key, dims, cuts, -0.22, 0.18) * values
    return jnp.clip(values, min=-limit, max=limit).astype(kind)


def setup_inputs(seed: int = 0) -> dict:
    splits = jax.random.split(jax.random.key(seed), 6)
    return {
        "tracers": draw_tracers(jax.random.fold_in(splits[5], 71), 0),
        "east_velocity": scatter_about(splits[1], (KZ, NLAT, NLON), 1.5, 6.0, ((1, 32), (2, 8))),
        "north_velocity": scatter_about(splits[2], (KZ, NLAT, NLON), 1.5, 6.0, ((1, 32), (2, 8))),
        "column_levels": place_ends(jax.random.randint(splits[3], (NLAT, NLON), 0, KZ + 1), jax.random.fold_in(splits[3], 1), 0, KZ).astype(jnp.int32),
        "surface_term": jnp.clip(jnp.exp(math.log(2.0) - 3.6888794 * jax.random.uniform(splits[4], (NLAT, NLON), jnp.float32) ** level_of(splits[4], (NLAT, NLON), ((0, 32), (1, 8)), -0.2, 0.2)), 0.05, 2.0),
    }


time_step = 0.5
biharm_coef = 0.05
vertical_coef = 0.8

def to_east(field):
    return jnp.roll(field, -1, axis=-1)

def to_west(field):
    return jnp.roll(field, 1, axis=-1)

def to_north(field):
    return jnp.concatenate([field[..., 1:, :], jnp.zeros_like(field[..., :1, :])], axis=-2)

def to_south(field):
    return jnp.concatenate([jnp.zeros_like(field[..., :1, :]), field[..., :-1, :]], axis=-2)

def level_up(field):
    return jnp.concatenate([field[..., 1:, :, :], jnp.zeros_like(field[..., :1, :, :])], axis=-3)

def level_down(field):
    return jnp.concatenate([jnp.zeros_like(field[..., :1, :, :]), field[..., :-1, :, :]], axis=-3)

def laplace(field, ocean):
    total = to_east(ocean) * (to_east(field) - field) + to_west(ocean) * (to_west(field) - field)
    total = total + to_north(ocean) * (to_north(field) - field) + to_south(ocean) * (to_south(field) - field)
    return ocean * total

def transport(field, ocean, eastward, northward):
    east_flux = eastward * ocean * to_east(ocean) * (field + to_east(field)) * 0.5
    north_flux = northward * ocean * to_north(ocean) * (field + to_north(field)) * 0.5
    return -(east_flux - to_west(east_flux)) - (north_flux - to_south(north_flux))

def vertical(field, ocean):
    return ocean * (level_up(ocean) * (level_up(field) - field) + level_down(ocean) * (level_down(field) - field))

def tendency(field, ocean, eastward, northward):
    smooth = laplace(laplace(field, ocean), ocean)
    return ocean * (transport(field, ocean, eastward, northward) - biharm_coef * smooth + vertical_coef * vertical(field, ocean))

def nine_point(pressure, surface, diagonal):
    edges = to_east(surface) * to_east(pressure) + to_west(surface) * to_west(pressure)
    edges = edges + to_north(surface) * to_north(pressure) + to_south(surface) * to_south(pressure)
    corners = to_north(to_east(surface)) * to_north(to_east(pressure)) + to_north(to_west(surface)) * to_north(to_west(pressure))
    corners = corners + to_south(to_east(surface)) * to_south(to_east(pressure)) + to_south(to_west(surface)) * to_south(to_west(pressure))
    return diagonal * pressure - surface * (edges + 0.5 * corners)

def reference(tracers, east_velocity, north_velocity, column_levels, surface_term):
    ocean = (jnp.arange(KZ)[:, None, None] < column_levels[None]).astype(jnp.float32)
    eastward = east_velocity.astype(jnp.float32)
    northward = north_velocity.astype(jnp.float32)
    first = tendency(tracers, ocean, eastward, northward)
    middle = tracers + time_step * first
    second = tendency(middle, ocean, eastward, northward)
    updated = tracers + 0.5 * time_step * (first + second)
    surface = ocean[0]
    forcing = lax.optimization_barrier(jnp.sum(ocean * (updated[0] - 0.5 * updated[1]), axis=0)) / math.sqrt(KZ)
    diagonal = 6.0 + surface_term
    pressure = jnp.zeros_like(forcing)
    resid = forcing
    precond = resid / diagonal
    direction = precond
    product_now = jnp.sum(resid * precond)
    for iteration in range(ITERS):
        image = nine_point(direction, surface, diagonal)
        alpha = product_now / jnp.sum(direction * image)
        pressure = pressure + alpha * direction
        resid = resid - alpha * image
        precond = resid / diagonal
        product_next = jnp.sum(resid * precond)
        direction = precond + product_next / product_now * direction
        product_now = product_next
    east_slope = surface * to_east(surface) * (to_east(pressure) - pressure)
    north_slope = surface * to_north(surface) * (to_north(pressure) - pressure)
    return (updated, jnp.stack([east_slope, north_slope]))
```

```python
import functools
import math

import jax
import jax.numpy as jnp
from jax import lax
from jax.experimental import pallas as pl
from jax.experimental.pallas import tpu as pltpu
from jax.sharding import PartitionSpec as P

MESH = pl.DeviceIdType.MESH
F32 = jnp.float32
BF16 = jnp.bfloat16

ITERS = 4
LEVELS = 32
ROWS = 16
HALO = 4
HIGH = ROWS + 2 * HALO
NX = 4
NZ = 2

time_step = 0.5
biharm_coef = 0.05
vertical_coef = 0.8


def iota(shape, axis):
    return lax.broadcasted_iota(jnp.int32, shape, axis)


def kernel(
    lats, lons, trc, vel_e, vel_n, levels_in, term_in, upd, grad,
    tin, vin, vf, levi, termi, X, M, LP, V, Xs, Ms, LPs, Us, Vs, Qt, Qv, pack, pack_in, corner_in,
    xb, xb_in, vbn, vbs, vbn_in, vbs_in, FL, frn, frs, fre, frw, fc,
    FO, gn, gs, ge, gw, gc, MK, FS, tout, sa, ra, sb, rb,
    in_sem, out_sem, s1, r1, s2, r2, sas, sar, sbs, sbr,
):
    la, lo = lax.axis_index("lat"), lax.axis_index("lon")
    north, south = lax.rem(la + 1, lats), lax.rem(la + lats - 1, lats)
    east, west = lax.rem(lo + 1, lons), lax.rem(lo + lons - 1, lons)
    ny = lats // (NX * NZ)
    y, zx = la // (NX * NZ), lax.rem(la, NX * NZ)
    zz, xx = zx // NX, lax.rem(zx, NX)
    size_a, size_b = ny * NX, NZ * lons
    me_a, me_b = y * NX + xx, zz * lons + lo

    def partner_a(k):
        a = lax.rem(me_a + k, size_a)
        return ((a // NX) * NZ + zz) * NX + lax.rem(a, NX), lo

    def partner_b(k):
        b = lax.rem(me_b + k, size_b)
        return (y * NZ + b // lons) * NX + xx, lax.rem(b, lons)

    loads = []
    for h in range(2):
        loads.append(pltpu.make_async_copy(trc.at[:, pl.ds(128 * h, 128)], tin.at[h], in_sem.at[h]))
    for w, src in enumerate((vel_e, vel_n)):
        for h in range(2):
            loads.append(pltpu.make_async_copy(src.at[:, pl.ds(128 * h, 128)], vin.at[w, h], in_sem.at[2 + 2 * w + h]))
    loads.append(pltpu.make_async_copy(levels_in, levi, in_sem.at[6]))
    loads.append(pltpu.make_async_copy(term_in, termi, in_sem.at[7]))
    for load in loads:
        load.start()

    barrier = pltpu.get_barrier_semaphore()
    around = [
        (north, lo), (south, lo), (la, east), (la, west),
        (north, east), (south, east), (north, west), (south, west),
    ]
    partners = [partner_a(k) for k in range(1, size_a)] + [partner_b(k) for k in range(1, size_b)]
    for device in around + partners:
        pl.semaphore_signal(barrier, inc=1, device_id=device, device_id_type=MESH)

    def send(src, dst, k, device, ss=s1, rr=r1):
        copy = pltpu.make_async_remote_copy(
            src_ref=src, dst_ref=dst, send_sem=ss.at[k], recv_sem=rr.at[k], device_id=device, device_id_type=MESH
        )
        copy.start()
        return copy

    lane = iota((8, 128), 1)
    sub = iota((8, 128), 0)
    lane16 = lax.rem(lane, 16)
    laneq = lane // 16

    loads[0].wait()
    loads[1].wait()

    def fill_x(r, carry):
        for h in range(2):
            X[r + HALO, h] = tin[h, pl.ds(r, 64, stride=ROWS), :]
        return carry

    lax.fori_loop(0, ROWS, fill_x, 0)
    for j in range(2):
        xb[0, j] = X[16 + j].astype(BF16)
        xb[1, j] = X[6 + j].astype(BF16)

    loads[6].wait()
    loads[7].wait()
    for h in range(2):
        for tile in range(2):
            FL[h, tile, 0] = levi[8 * tile : 8 * tile + 8, 128 * h : 128 * h + 128].astype(F32)
            FL[h, tile, 1] = termi[8 * tile : 8 * tile + 8, 128 * h : 128 * h + 128]

    pl.semaphore_wait(barrier, len(around) + len(partners))

    c_rows = [
        send(X.at[pl.ds(18, 2)], X.at[pl.ds(2, 2)], 0, (north, lo)),
        send(X.at[pl.ds(4, 2)], X.at[pl.ds(20, 2)], 2, (south, lo)),
        send(xb.at[0], xb_in.at[0], 1, (north, lo)),
        send(xb.at[1], xb_in.at[1], 3, (south, lo)),
    ]
    c_flat = [
        send(FL.at[:, 1], frs, 13, (north, lo)),
        send(FL.at[:, 0], frn, 14, (south, lo)),
        send(FL.at[1], frw, 15, (la, east)),
        send(FL.at[0], fre, 16, (la, west)),
        send(FL.at[1, 1], fc.at[0], 17, (north, east)),
        send(FL.at[1, 0], fc.at[1], 18, (south, east)),
        send(FL.at[0, 1], fc.at[2], 19, (north, west)),
        send(FL.at[0, 0], fc.at[3], 20, (south, west)),
    ]

    for load in loads[2:6]:
        load.wait()

    def widen(n, carry):
        at = pl.ds(pl.multiple_of(64 * n, 64), 64)
        for w in range(2):
            for h in range(2):
                vf[w, h, at, :] = vin[w, h, at, :].astype(F32) * 0.5
        return carry

    lax.fori_loop(0, 8, widen, 0)

    def fill_v(r, carry):
        for w in range(2):
            for h in range(2):
                V[r + HALO, w, h] = vf[w, h, pl.ds(r, 32, stride=ROWS), :]
        return carry

    lax.fori_loop(0, ROWS, fill_v, 0)
    for j in range(3):
        vbn[j] = V[17 + j].astype(BF16)
    for j in range(2):
        vbs[j] = V[4 + j].astype(BF16)
    c_vel = [
        send(vbn.at[pl.ds(1, 2)], vbn_in.at[pl.ds(1, 2)], 4, (north, lo)),
        send(vbn.at[0, 1], vbn_in.at[0, 1], 5, (north, lo)),
        send(vbs, vbs_in, 6, (south, lo)),
    ]

    def seam_of(parts):
        out = jnp.zeros((8, 128), F32)
        for q, (low, high) in enumerate(parts):
            both = jnp.where(lane >= 124, high, low)
            out = jnp.where(laneq == q, pltpu.roll(both, (16 * q + 4) % 128, 1), out)
        return out

    def seam_x(i):
        return seam_of([(X[i, 0, 8 * q : 8 * q + 8, :], X[i, 1, 8 * q : 8 * q + 8, :]) for q in range(8)])

    def seam_v(i):
        return seam_of(
            [
                (V[i, q // 4, 0, 8 * (q % 4) : 8 * (q % 4) + 8, :], V[i, q // 4, 1, 8 * (q % 4) : 8 * (q % 4) + 8, :])
                for q in range(8)
            ]
        )

    def pack_rows(r, carry):
        Qt[r] = seam_x(r + HALO)
        Qv[r] = seam_v(r + HALO)
        return carry

    lax.fori_loop(0, ROWS, pack_rows, 0)
    for a in range(4):
        for w, Q in enumerate((Qt, Qv)):
            for side in range(2):
                out = jnp.zeros((8, 128), F32)
                for n in range(4):
                    turn = (4 * n - 4 * side) % 128
                    out = jnp.where(lane16 // 4 == n, pltpu.roll(Q[4 * a + n], turn, 1) if turn else Q[4 * a + n], out)
                pack[side, a, w] = out
    c_seam = [
        send(pack.at[0], pack_in.at[0], 7, (la, east)),
        send(pack.at[1], pack_in.at[1], 8, (la, west)),
        send(pack.at[0, 3], corner_in.at[0], 9, (north, east)),
        send(pack.at[0, 0], corner_in.at[1], 10, (south, east)),
        send(pack.at[1, 3], corner_in.at[2], 11, (north, west)),
        send(pack.at[1, 0], corner_in.at[3], 12, (south, west)),
    ]

    def flat(own, n, s, e, w, ne, se, nw, sw):
        parts = [jnp.concatenate([own[h][0], own[h][1], jnp.where(sub < 4, n[h], s[h])], axis=0) for h in range(2)]
        right = jnp.concatenate([e[0], e[1], jnp.where(sub < 4, ne, se)], axis=0)
        left = jnp.concatenate([w[0], w[1], jnp.where(sub < 4, nw, sw)], axis=0)
        parts.append(jnp.where(iota((24, 128), 1) < 64, right, left))
        return parts

    def to_east(parts):
        rolled = [pltpu.roll(p, 127, 1) for p in parts]
        last = iota(parts[0].shape, 1) == 127
        return [jnp.where(last, rolled[(k + 1) % 3], rolled[k]) for k in range(3)]

    def to_west(parts):
        rolled = [pltpu.roll(p, 1, 1) for p in parts]
        first = iota(parts[0].shape, 1) == 0
        return [jnp.where(first, rolled[(k + 2) % 3], rolled[k]) for k in range(3)]

    def to_north(part):
        return pltpu.roll(part, 23, 0)

    def to_south(part):
        return pltpu.roll(part, 1, 0)

    for copy in c_flat:
        copy.wait()

    def flat_field(f):
        return flat(
            [[FL[h, tile, f] for tile in range(2)] for h in range(2)],
            [frn[h, f] for h in range(2)], [frs[h, f] for h in range(2)],
            [fre[tile, f] for tile in range(2)], [frw[tile, f] for tile in range(2)],
            fc[3, f], fc[2, f], fc[1, f], fc[0, f],
        )

    row = iota((24, 128), 0)
    past_north = jnp.logical_and(row >= 16, row < 20).astype(jnp.int32) * (la == lats - 1).astype(jnp.int32)
    past_south = (row >= 20).astype(jnp.int32) * (la == 0).astype(jnp.int32)
    outside = (past_north + past_south) > 0
    depth = [jnp.where(outside, 0.0, p) for p in flat_field(0)]
    diagonal = [6.0 + p for p in flat_field(1)]

    wide = iota((24, 128), 1)
    seam_e = jnp.where(wide >= 124, depth[1], depth[2])
    seam_w = jnp.where(wide >= 124, depth[2], depth[0])
    base = jnp.where(wide < 8, pltpu.roll(seam_e, 4, 1), pltpu.roll(seam_w, 12, 1))
    base = jnp.where(wide < 16, base, 0.0)
    for turn in (16, 32, 64):
        base = base + pltpu.roll(base, turn, 1)
    east_depth = to_east(depth) + [pltpu.roll(base, 127, 1)]
    west_depth = to_west(depth) + [pltpu.roll(base, 1, 1)]
    for slot, p in enumerate((0, 1, 3)):
        own = (depth + [base])[p]
        MK[slot, 0] = own
        MK[slot, 1] = jnp.minimum(own, east_depth[p])
        MK[slot, 2] = jnp.minimum(own, west_depth[p])
        MK[slot, 3] = jnp.minimum(own, to_north(own))
        MK[slot, 4] = jnp.minimum(own, to_south(own))

    for copy in c_rows + c_vel + c_seam:
        copy.wait()
    for j in range(2):
        X[j] = xb_in[0, j].astype(F32)
        X[22 + j] = xb_in[1, j].astype(F32)
        V[2 + j] = vbn_in[1 + j].astype(F32)
        V[20 + j] = vbs_in[j].astype(F32)
    V[1, 1] = vbn_in[0, 1].astype(F32)

    def seam_row(own, from_east, from_west, n):
        out = jnp.where(lane16 < 4, own, pltpu.roll(own, 8, 1))
        right = pltpu.roll(from_east, (4 - 4 * n) % 128, 1) if n != 1 else from_east
        left = pltpu.roll(from_west, (8 - 4 * n) % 128, 1) if n != 2 else from_west
        out = jnp.where(lane16 // 4 == 1, right, out)
        return jnp.where(lane16 // 4 == 2, left, out)

    def put_velocity(i, both):
        other = pltpu.roll(both, 64, 1)
        Us[i] = jnp.where(lane < 64, both, other)
        Vs[i] = jnp.where(lane < 64, other, both)

    for a in range(4):
        for n in range(4):
            i = HALO + 4 * a + n
            Xs[i] = seam_row(Qt[4 * a + n], pack_in[1, a, 0], pack_in[0, a, 0], n)
            put_velocity(i, seam_row(Qv[4 * a + n], pack_in[1, a, 1], pack_in[0, a, 1], n))
    for n in range(4):
        Xs[n] = seam_row(seam_x(n), corner_in[2, 0], corner_in[0, 0], n)
        Xs[20 + n] = seam_row(seam_x(20 + n), corner_in[3, 0], corner_in[1, 0], n)
        if n > 0:
            put_velocity(n, seam_row(seam_v(n), corner_in[2, 1], corner_in[0, 1], n))
        if n < 2:
            put_velocity(20 + n, seam_row(seam_v(20 + n), corner_in[3, 1], corner_in[1, 1], n))

    level = iota((LEVELS, 128), 0).astype(F32)
    level_s = (sub + 8 * lax.rem(laneq, 4)).astype(F32)
    lane_f = iota((LEVELS, 128), 1)

    def mask_row(slot, n, i):
        return MK[slot, n, pl.ds(lax.rem(i + 20, 24), 1), :]

    def pull(seam, t, src, dst):
        return jnp.concatenate(
            [pltpu.roll(seam, (dst - 16 * (4 * t + g) - src) % 128, 1) for g in range(4)], axis=0
        )

    def shift_e(halves, seam, t):
        low, high = pltpu.roll(halves[0], 127, 1), pltpu.roll(halves[1], 127, 1)
        return [jnp.where(lane_f == 127, high, low), jnp.where(lane_f == 127, pull(seam, t, 4, 127), high)]

    def shift_w(halves, seam, t):
        low, high = pltpu.roll(halves[0], 1, 1), pltpu.roll(halves[1], 1, 1)
        return [jnp.where(lane_f == 0, pull(seam, t, 11, 0), low), jnp.where(lane_f == 0, low, high)]

    def at(ref, i, h, t):
        return ref[i, h, 32 * t : 32 * t + 32, :]

    def laplace(ref, seams, first, last):
        def step(i, carry):
            seam = seams[i]
            for t in range(2):
                x = [at(ref, i, h, t) for h in range(2)]
                xe, xw = shift_e(x, seam, t), shift_w(x, seam, t)
                for h in range(2):
                    total = jnp.where(level < mask_row(h, 1, i), xe[h] - x[h], 0.0)
                    total += jnp.where(level < mask_row(h, 2, i), xw[h] - x[h], 0.0)
                    total += jnp.where(level < mask_row(h, 3, i), at(ref, i + 1, h, t) - x[h], 0.0)
                    total += jnp.where(level < mask_row(h, 4, i), at(ref, i - 1, h, t) - x[h], 0.0)
                    LP[i, h, 32 * t : 32 * t + 32, :] = total
            total = jnp.where(level_s < mask_row(2, 1, i), pltpu.roll(seam, 127, 1) - seam, 0.0)
            total += jnp.where(level_s < mask_row(2, 2, i), pltpu.roll(seam, 1, 1) - seam, 0.0)
            total += jnp.where(level_s < mask_row(2, 3, i), seams[i + 1] - seam, 0.0)
            total += jnp.where(level_s < mask_row(2, 4, i), seams[i - 1] - seam, 0.0)
            LPs[i] = total
            return carry

        lax.fori_loop(first, last, step, 0)

    def north_flux(ref, seams, i):
        flux = []
        for t in range(2):
            for h in range(2):
                value = V[i, 1, h] * (at(ref, i, h, t) + at(ref, i + 1, h, t))
                value += biharm_coef * (at(LP, i + 1, h, t) - at(LP, i, h, t))
                flux.append(jnp.where(level < mask_row(h, 3, i), value, 0.0))
        value = Vs[i] * (seams[i] + seams[i + 1]) + biharm_coef * (LPs[i + 1] - LPs[i])
        flux.append(jnp.where(level_s < mask_row(2, 3, i), value, 0.0))
        return flux

    def tendency(ref, seams, first, last, put, put_seam):
        def step(i, below):
            above = north_flux(ref, seams, i)
            seam = seams[i]
            value = Us[i] * (seam + pltpu.roll(seam, 127, 1)) + biharm_coef * (pltpu.roll(LPs[i], 127, 1) - LPs[i])
            flux_s = jnp.where(level_s < mask_row(2, 1, i), value, 0.0)
            for t in range(2):
                x = [at(ref, i, h, t) for h in range(2)]
                lap = [at(LP, i, h, t) for h in range(2)]
                xe, lape = shift_e(x, seam, t), shift_e(lap, LPs[i], t)
                flux = []
                for h in range(2):
                    value = V[i, 0, h] * (x[h] + xe[h]) + biharm_coef * (lape[h] - lap[h])
                    flux.append(jnp.where(level < mask_row(h, 1, i), value, 0.0))
                flux_w = shift_w(flux, flux_s, t)
                for h in range(2):
                    up = jnp.where(level + 1.0 < mask_row(h, 0, i), pltpu.roll(x[h], LEVELS - 1, 0) - x[h], 0.0)
                    total = (flux_w[h] - flux[h]) + (below[2 * t + h] - above[2 * t + h])
                    total += vertical_coef * (up - pltpu.roll(up, 1, 0))
                    put(i, t, h, x[h], total)
            if put_seam is not None:
                turned = pltpu.roll(seam, 112, 1)
                upper = jnp.where(sub < 7, pltpu.roll(seam, 7, 0), pltpu.roll(turned, 7, 0))
                up = jnp.where(level_s + 1.0 < mask_row(2, 0, i), upper - seam, 0.0)
                turned = pltpu.roll(up, 16, 1)
                down = jnp.where(sub > 0, pltpu.roll(up, 1, 0), pltpu.roll(turned, 1, 0))
                total = (pltpu.roll(flux_s, 1, 1) - flux_s) + (below[4] - above[4]) + vertical_coef * (up - down)
                put_seam(i, seam, total)
            return above

        lax.fori_loop(first, last, step, north_flux(ref, seams, first - 1))

    def put_middle(i, t, h, x, total):
        M[i, h, 32 * t : 32 * t + 32, :] = x + time_step * total

    def put_middle_seam(i, x, total):
        Ms[i] = x + time_step * total

    laplace(X, Xs, 1, 23)
    tendency(X, Xs, 2, 22, put_middle, put_middle_seam)

    def put_updated(i, t, h, m, total):
        value = 0.5 * (at(X, i, h, t) + m) + 0.5 * time_step * total
        tout[h, pl.ds(512 * t + i - HALO, 32, stride=ROWS), :] = value
        part = jnp.where(level < mask_row(h, 0, i), value, 0.0)
        part = (part[0:8] + part[8:16]) + (part[16:24] + part[24:32])
        if t == 0:
            FS[i - HALO, h] = part
        else:
            FS[i - HALO, h] = FS[i - HALO, h] - 0.5 * part

    laplace(M, Ms, 3, 21)
    tendency(M, Ms, 4, 20, put_updated, None)

    stores = [
        pltpu.make_async_copy(tout.at[h], upd.at[:, pl.ds(128 * h, 128)], out_sem.at[h]) for h in range(2)
    ]
    for store in stores:
        store.start()

    for h in range(2):
        for tile in range(2):
            FO[h, tile] = jnp.sum(FS[8 * tile : 8 * tile + 8, h], axis=1) * (1.0 / math.sqrt(LEVELS))
    c_forcing = [
        send(FO.at[:, 1], gs, 0, (north, lo), s2, r2),
        send(FO.at[:, 0], gn, 1, (south, lo), s2, r2),
        send(FO.at[1], gw, 2, (la, east), s2, r2),
        send(FO.at[0], ge, 3, (la, west), s2, r2),
        send(FO.at[1, 1], gc.at[0], 4, (north, east), s2, r2),
        send(FO.at[1, 0], gc.at[1], 5, (south, east), s2, r2),
        send(FO.at[0, 1], gc.at[2], 6, (north, west), s2, r2),
        send(FO.at[0, 0], gc.at[3], 7, (south, west), s2, r2),
    ]
    surface = [p > 0.0 for p in depth]
    inverse = [jnp.where(surface[k], 1.0 / diagonal[k], 0.0) for k in range(3)]
    own_row = row < 16
    weight = [jnp.where(own_row, diagonal[k], 0.0) for k in range(2)]
    for copy in c_forcing:
        copy.wait()
    forcing = flat(
        [[FO[h, tile] for tile in range(2)] for h in range(2)],
        [gn[h] for h in range(2)], [gs[h] for h in range(2)],
        [ge[tile] for tile in range(2)], [gw[tile] for tile in range(2)],
        gc[3], gc[2], gc[1], gc[0],
    )

    def apply_b(parts):
        columns = [to_north(p) + to_south(p) for p in parts]
        mixed = [p + 0.5 * c for p, c in zip(parts, columns)]
        e, w = to_east(mixed), to_west(mixed)
        return [inverse[k] * (columns[k] + e[k] + w[k]) for k in range(3)]

    basis = [[forcing[k] * inverse[k] for k in range(3)]]
    basis.append(apply_b(basis[0]))
    for j in range(2, ITERS + 1):
        image = apply_b(basis[j - 1])
        basis.append([2.0 * image[k] - basis[j - 2][k] for k in range(3)])

    def partial(left, right):
        total = left[0] * right[0] + left[1] * right[1]
        total = total[0:8] + total[8:16]
        return jnp.sum(total, axis=0, keepdims=True)

    rows = []
    for j in range(ITERS):
        weighted = [weight[k] * basis[j][k] for k in range(2)]
        rows.append(partial(weighted, basis[j]))
        rows.append(partial(weighted, basis[j + 1]))
    sa[...] = jnp.concatenate(rows, axis=0)

    def gather(src, dst, me, size, partner, ss, rr):
        copies = []
        for k in range(1, size):
            copy = pltpu.make_async_remote_copy(
                src_ref=src, dst_ref=dst.at[me], send_sem=ss.at[k], recv_sem=rr.at[me],
                device_id=partner(k), device_id_type=MESH,
            )
            copy.start()
            copies.append(copy)
        dst[me] = src[...]
        for k in range(1, size):
            copies[k - 1].wait_send()
            other = lax.rem(me + k, size)
            pltpu.make_async_remote_copy(
                src_ref=src, dst_ref=dst.at[other], send_sem=ss.at[k], recv_sem=rr.at[other],
                device_id=partner(k), device_id_type=MESH,
            ).wait_recv()
        parts = [dst[k] for k in range(size)]
        while len(parts) > 1:
            parts = [parts[k] + parts[k + 1] for k in range(0, len(parts) - 1, 2)] + parts[len(parts) - len(parts) % 2 :]
        return parts[0]

    sb[...] = gather(sa, ra, me_a, size_a, partner_a, sas, sar)
    total = gather(sb, rb, me_b, size_b, partner_b, sbs, sbr)
    total = jnp.broadcast_to(jnp.sum(total, axis=1, keepdims=True), (8, 128))
    inner = [total[k : k + 1, :] for k in range(8)]
    c = inner[:2] + [2.0 * inner[k] - inner[k % 2] for k in range(2, 8)]

    def gram(i, j):
        return 0.5 * (c[i + j] + c[abs(i - j)])

    def ratio(top, bottom):
        good = jnp.logical_and(bottom > 0.0, top > 0.0)
        return jnp.where(good, top / jnp.where(good, bottom, 1.0), 0.0)

    zero = jnp.zeros_like(c[0])
    resid = [jnp.ones_like(zero)]
    direction = list(resid)
    pressure = [zero] * ITERS
    product = c[0]
    for k in range(ITERS):
        image = list(direction) + [zero]
        for j, value in enumerate(direction):
            if j == 0:
                image[1] = image[1] - value
            else:
                image[j + 1] = image[j + 1] - 0.5 * value
                image[j - 1] = image[j - 1] - 0.5 * value
        bottom = zero
        for i, value in enumerate(direction):
            line = zero
            for j, other in enumerate(image):
                line = line + other * gram(i, j)
            bottom = bottom + value * line
        alpha = ratio(product, bottom)
        for j, value in enumerate(direction):
            pressure[j] = pressure[j] + alpha * value
        if k + 1 < ITERS:
            resid = [a - alpha * b for a, b in zip(resid + [zero], image)]
            following = zero
            for i, value in enumerate(resid):
                line = zero
                for j, other in enumerate(resid):
                    line = line + other * gram(i, j)
                following = following + value * line
            beta = ratio(following, product)
            direction = [a + beta * b for a, b in zip(resid, direction + [zero])]
            product = following

    field = []
    for k in range(3):
        value = pressure[0] * basis[0][k]
        for j in range(1, ITERS):
            value = value + pressure[j] * basis[j][k]
        field.append(value)
    field_e = to_east(field)
    wet = [jnp.where(surface[k], 1.0, 0.0) for k in range(3)]
    wet_e = to_east(wet)
    for h in range(2):
        slope_e = wet[h] * wet_e[h] * (field_e[h] - field[h])
        slope_n = wet[h] * to_north(wet[h]) * (to_north(field[h]) - field[h])
        grad[0, :, 128 * h : 128 * h + 128] = slope_e[0:16]
        grad[1, :, 128 * h : 128 * h + 128] = slope_n[0:16]
    for store in stores:
        store.wait()


def body(lats, lons, tracers, east_velocity, north_velocity, column_levels, surface_term):
    tall = 2 * LEVELS * ROWS
    cells = tracers.reshape(tall, 256)
    east = east_velocity.reshape(LEVELS * ROWS, 256)
    north = north_velocity.reshape(LEVELS * ROWS, 256)
    size_a, size_b = lats // NZ, NZ * lons
    vmem = pltpu.VMEM
    scratch = [
        vmem((2, tall, 128), F32),
        vmem((2, 2, LEVELS * ROWS, 128), BF16),
        vmem((2, 2, LEVELS * ROWS, 128), F32),
        vmem((ROWS, 256), jnp.int32),
        vmem((ROWS, 256), F32),
        vmem((HIGH, 2, 64, 128), F32),
        vmem((HIGH, 2, 64, 128), F32),
        vmem((HIGH, 2, 64, 128), F32),
        vmem((HIGH, 2, 2, LEVELS, 128), F32),
        vmem((HIGH, 8, 128), F32),
        vmem((HIGH, 8, 128), F32),
        vmem((HIGH, 8, 128), F32),
        vmem((HIGH, 8, 128), F32),
        vmem((HIGH, 8, 128), F32),
        vmem((ROWS, 8, 128), F32),
        vmem((ROWS, 8, 128), F32),
        vmem((2, 4, 2, 8, 128), F32),
        vmem((2, 4, 2, 8, 128), F32),
        vmem((4, 2, 8, 128), F32),
        vmem((2, 2, 2, 64, 128), BF16),
        vmem((2, 2, 2, 64, 128), BF16),
        vmem((3, 2, 2, LEVELS, 128), BF16),
        vmem((2, 2, 2, LEVELS, 128), BF16),
        vmem((3, 2, 2, LEVELS, 128), BF16),
        vmem((2, 2, 2, LEVELS, 128), BF16),
        vmem((2, 2, 2, 8, 128), F32),
        vmem((2, 2, 8, 128), F32),
        vmem((2, 2, 8, 128), F32),
        vmem((2, 2, 8, 128), F32),
        vmem((2, 2, 8, 128), F32),
        vmem((4, 2, 8, 128), F32),
        vmem((2, 2, 8, 128), F32),
        vmem((2, 8, 128), F32),
        vmem((2, 8, 128), F32),
        vmem((2, 8, 128), F32),
        vmem((2, 8, 128), F32),
        vmem((4, 8, 128), F32),
        vmem((3, 5, HIGH, 128), F32),
        vmem((ROWS, 2, 8, 128), F32),
        vmem((2, tall, 128), F32),
        vmem((8, 128), F32),
        vmem((size_a, 8, 128), F32),
        vmem((8, 128), F32),
        vmem((size_b, 8, 128), F32),
        pltpu.SemaphoreType.DMA((8,)),
        pltpu.SemaphoreType.DMA((2,)),
        pltpu.SemaphoreType.DMA((21,)),
        pltpu.SemaphoreType.DMA((21,)),
        pltpu.SemaphoreType.DMA((8,)),
        pltpu.SemaphoreType.DMA((8,)),
        pltpu.SemaphoreType.DMA((size_a,)),
        pltpu.SemaphoreType.DMA((size_a,)),
        pltpu.SemaphoreType.DMA((size_b,)),
        pltpu.SemaphoreType.DMA((size_b,)),
    ]
    hbm = pl.BlockSpec(memory_space=pl.ANY)
    updated, gradient = pl.pallas_call(
        functools.partial(kernel, lats, lons),
        out_shape=(jax.ShapeDtypeStruct((tall, 256), F32), jax.ShapeDtypeStruct((2, ROWS, 256), F32)),
        in_specs=[hbm] * 5,
        out_specs=(hbm, pl.BlockSpec(memory_space=pltpu.VMEM)),
        scratch_shapes=scratch,
        compiler_params=pltpu.CompilerParams(
            collective_id=0, has_side_effects=True, vmem_limit_bytes=48 * 1024 * 1024
        ),
    )(cells, east, north, column_levels, surface_term)
    return updated.reshape(2, LEVELS, ROWS, 256), gradient


def solution(mesh):
    in_specs = (
        P(None, None, "lat", "lon"),
        P(None, "lat", "lon"),
        P(None, "lat", "lon"),
        P("lat", "lon"),
        P("lat", "lon"),
    )
    out_specs = (P(None, None, "lat", "lon"), P(None, "lat", "lon"))
    step = functools.partial(body, mesh.shape["lat"], mesh.shape["lon"])
    return jax.shard_map(step, mesh=mesh, in_specs=in_specs, out_specs=out_specs, check_vma=False)
```

```python
import functools
import math

import jax
import jax.numpy as jnp
from jax import lax
from jax.experimental import pallas as pl
from jax.experimental.pallas import tpu as pltpu
from jax.sharding import PartitionSpec as P

MESH = pl.DeviceIdType.MESH
F32 = jnp.float32
BF16 = jnp.bfloat16

ITERS = 4
LEVELS = 32
ROWS = 16
HALO = 4
HIGH = ROWS + 2 * HALO
NX = 4
NZ = 2

time_step = 0.5
biharm_coef = 0.05
vertical_coef = 0.8


def iota(shape, axis):
    return lax.broadcasted_iota(jnp.int32, shape, axis)


def kernel(
    lats, lons, trc, vel_e, vel_n, levels_in, term_in, out, grad,
    vin, vf, levi, termi, X, M, LP, SX, V, U, Xs, Ms, Us, Vs, Qt, Qv, pack, pack_in, corner_in,
    xb, xb_in, vbn, vbs, vbn_in, vbs_in, FL, FT, ft_in,
    FO, gn, gs, ge, gw, gc, MK, FS, tout, sa, ra, sb, rb,
    in_sem, s1, r1, s2, r2, sas, sar, sbs, sbr,
):
    la, lo = lax.axis_index("lat"), lax.axis_index("lon")
    north, south = lax.rem(la + 1, lats), lax.rem(la + lats - 1, lats)
    east, west = lax.rem(lo + 1, lons), lax.rem(lo + lons - 1, lons)
    ny = lats // (NX * NZ)
    y, zx = la // (NX * NZ), lax.rem(la, NX * NZ)
    zz, xx = zx // NX, lax.rem(zx, NX)
    size_a, size_b = ny * NX, NZ * lons
    me_a, me_b = y * NX + xx, zz * lons + lo

    def partner_a(k):
        a = lax.rem(me_a + k, size_a)
        return ((a // NX) * NZ + zz) * NX + lax.rem(a, NX), lo

    def partner_b(k):
        b = lax.rem(me_b + k, size_b)
        return (y * NZ + b // lons) * NX + xx, lax.rem(b, lons)

    loads = [
        pltpu.make_async_copy(levels_in, levi, in_sem.at[0]),
        pltpu.make_async_copy(term_in, termi, in_sem.at[1]),
    ]
    edge_rows = [0, 1, 2, 3, 12, 13, 14, 15]
    inner_rows = list(range(4, 12))

    def load_rows(rows):
        return [
            pltpu.make_async_copy(
                trc.at[:, r, pl.ds(128 * h, 128)], X.at[r + HALO, h, pl.ds(8, 64)], in_sem.at[6 + 2 * r + h]
            )
            for r in rows
            for h in range(2)
        ]

    x_loads = load_rows(edge_rows)
    v_loads = [
        pltpu.make_async_copy(src.at[:, pl.ds(128 * h, 128)], vin.at[w, h], in_sem.at[2 + 2 * w + h])
        for w, src in enumerate((vel_e, vel_n))
        for h in range(2)
    ]
    y_loads = load_rows(inner_rows)
    for load in loads + x_loads + v_loads + y_loads:
        load.start()

    barrier = pltpu.get_barrier_semaphore()
    around = [
        (north, lo), (south, lo), (la, east), (la, west),
        (north, east), (south, east), (north, west), (south, west),
    ]
    partners = [partner_a(k) for k in range(1, size_a)] + [partner_b(k) for k in range(1, size_b)]
    for device in around + partners:
        pl.semaphore_signal(barrier, inc=1, device_id=device, device_id_type=MESH)

    def send(src, dst, k, device, ss=s1, rr=r1):
        copy = pltpu.make_async_remote_copy(
            src_ref=src, dst_ref=dst, send_sem=ss.at[k], recv_sem=rr.at[k], device_id=device, device_id_type=MESH
        )
        copy.start()
        return copy

    lane = iota((8, 128), 1)
    sub = iota((8, 128), 0)
    lane16 = lax.rem(lane, 16)
    laneq = lane // 16

    def row_pairs(first, last, step, carry=0):
        def pair(n, carry):
            return step(first + 2 * n + 1, step(first + 2 * n, carry))

        return lax.fori_loop(0, (last - first) // 2, pair, carry)

    for load in loads:
        load.wait()
    for h in range(2):
        for tile in range(2):
            FL[h, tile, 0] = levi[8 * tile : 8 * tile + 8, 128 * h : 128 * h + 128].astype(F32)
            FL[h, tile, 1] = termi[8 * tile : 8 * tile + 8, 128 * h : 128 * h + 128]

    for h in range(2):
        FT[0, h] = jnp.where(sub < 4, pltpu.roll(FL[h, 1, 0], 4, 0), FL[h, 1, 1])
        FT[1, h] = jnp.where(sub < 4, FL[h, 0, 0], pltpu.roll(FL[h, 0, 1], 4, 0))
    for side in range(2):
        packed = jnp.zeros((8, 128), F32)
        for f in range(2):
            for tile in range(2):
                j = 2 * f + tile
                turn = (4 * j + 4) % 128 if side == 0 else 4 * j
                value = FL[1 - side, tile, f]
                packed = jnp.where(lane // 4 == j, pltpu.roll(value, turn, 1) if turn else value, packed)
        pack[side, 0] = packed
        pack[side, 9] = packed

    for load in x_loads:
        load.wait()
    for j in range(3):
        xb[0, j] = X[16 + j, :, 8:72, :].astype(BF16)
        xb[1, j] = X[5 + j, :, 8:72, :].astype(BF16)

    for load in v_loads:
        load.wait()

    def widen(n, carry):
        rows = pl.ds(pl.multiple_of(64 * n, 64), 64)
        for w in range(2):
            for h in range(2):
                vf[w, h, rows, :] = vin[w, h, rows, :].astype(F32) * (0.5 * time_step)
        return carry

    lax.fori_loop(0, 8, widen, 0)

    def fill_v(i, carry):
        for w in range(2):
            for h in range(2):
                V[i, w, h] = vf[w, h, pl.ds(i - HALO, 32, stride=ROWS), :]
        return carry

    row_pairs(HALO, HALO + ROWS, fill_v)
    for j in range(3):
        vbn[j] = V[17 + j].astype(BF16)
    for j in range(2):
        vbs[j] = V[4 + j].astype(BF16)

    def seam_of(parts):
        out = jnp.zeros((8, 128), F32)
        for q, (low, high) in enumerate(parts):
            both = jnp.where(lane >= 124, high, low)
            out = jnp.where(laneq == q, pltpu.roll(both, (16 * q + 4) % 128, 1), out)
        return out

    def seam_x(i):
        return seam_of([(X[i, 0, 8 * q + 8 : 8 * q + 16, :], X[i, 1, 8 * q + 8 : 8 * q + 16, :]) for q in range(8)])

    def seam_v(i):
        return seam_of(
            [
                (V[i, q // 4, 0, 8 * (q % 4) : 8 * (q % 4) + 8, :], V[i, q // 4, 1, 8 * (q % 4) : 8 * (q % 4) + 8, :])
                for q in range(8)
            ]
        )

    def pack_rows(i, carry):
        Qt[i - HALO] = seam_x(i)
        Qv[i - HALO] = seam_v(i)
        return carry

    for load in y_loads:
        load.wait()
    row_pairs(HALO, HALO + ROWS, pack_rows)
    for a in range(4):
        for w, Q in enumerate((Qt, Qv)):
            for side in range(2):
                packed = jnp.zeros((8, 128), F32)
                for n in range(4):
                    turn = (4 * n - 4 * side) % 128
                    value = Q[4 * a + n]
                    packed = jnp.where(lane16 // 4 == n, pltpu.roll(value, turn, 1) if turn else value, packed)
                pack[side, 1 + 2 * a + w] = packed

    pl.semaphore_wait(barrier, len(around) + len(partners))

    body_rows = pl.ds(8, 64)
    c_side = [
        send(pack.at[0, pl.ds(0, 9)], pack_in.at[0], 0, (la, east)),
        send(pack.at[1, pl.ds(0, 9)], pack_in.at[1], 1, (la, west)),
    ]
    c_far = [
        send(pack.at[0, pl.ds(7, 3)], corner_in.at[0], 2, (north, east)),
        send(pack.at[0, pl.ds(0, 3)], corner_in.at[1], 3, (south, east)),
        send(pack.at[1, pl.ds(7, 3)], corner_in.at[2], 4, (north, west)),
        send(pack.at[1, pl.ds(0, 3)], corner_in.at[3], 5, (south, west)),
        send(FT.at[0], ft_in.at[0], 6, (north, lo)),
        send(FT.at[1], ft_in.at[1], 7, (south, lo)),
        send(X.at[19, :, body_rows], X.at[3, :, body_rows], 8, (north, lo)),
        send(X.at[4, :, body_rows], X.at[20, :, body_rows], 9, (south, lo)),
        send(xb.at[0], xb_in.at[0], 10, (north, lo)),
        send(xb.at[1], xb_in.at[1], 11, (south, lo)),
        send(vbn.at[pl.ds(1, 2)], vbn_in.at[pl.ds(1, 2)], 12, (north, lo)),
        send(vbn.at[0, 1], vbn_in.at[0, 1], 13, (north, lo)),
        send(vbs, vbs_in, 14, (south, lo)),
    ]

    def flat(own, n, s, e, w, ne, se, nw, sw):
        parts = [jnp.concatenate([own[h][0], own[h][1], jnp.where(sub < 4, n[h], s[h])], axis=0) for h in range(2)]
        right = jnp.concatenate([e[0], e[1], jnp.where(sub < 4, ne, se)], axis=0)
        left = jnp.concatenate([w[0], w[1], jnp.where(sub < 4, nw, sw)], axis=0)
        parts.append(jnp.where(iota((24, 128), 1) < 64, right, left))
        return parts

    def to_east(parts):
        rolled = [pltpu.roll(p, 127, 1) for p in parts]
        last = iota(parts[0].shape, 1) == 127
        return [jnp.where(last, rolled[(k + 1) % 3], rolled[k]) for k in range(3)]

    def to_west(parts):
        rolled = [pltpu.roll(p, 1, 1) for p in parts]
        first = iota(parts[0].shape, 1) == 0
        return [jnp.where(first, rolled[(k + 2) % 3], rolled[k]) for k in range(3)]

    def to_north(part):
        return pltpu.roll(part, 23, 0)

    def to_south(part):
        return pltpu.roll(part, 1, 0)

    def put_masks(depth):
        east_depth = to_east(depth)
        for h in range(2):
            MK[h, 0] = depth[h]
            MK[h, 1] = jnp.minimum(depth[h], east_depth[h])
            MK[h, 2] = jnp.minimum(depth[h], to_north(depth[h]))

    dry = jnp.zeros((8, 128), F32)
    put_masks([jnp.concatenate([FL[h, 0, 0], FL[h, 1, 0], dry], axis=0) for h in range(2)] + [jnp.zeros((24, 128), F32)])

    level = iota((LEVELS, 128), 0).astype(F32)
    lane_f = iota((LEVELS, 128), 1)
    mixing = time_step * biharm_coef
    lifting = time_step * vertical_coef
    places = [(t, h) for t in range(2) for h in range(2)]

    def mask_row(h, n, i):
        return MK[h, n, pl.ds(jnp.where(i >= HALO, i - HALO, i + 20), 1), :]

    def at(ref, i, h, t, up=0):
        return ref[i, h, 8 + 32 * t + up : 40 + 32 * t + up, :]

    def bare(ref, i, h, t):
        return ref[i, h, 32 * t : 32 * t + 32, :]

    def shift_e(halves):
        low, high = pltpu.roll(halves[0], 127, 1), pltpu.roll(halves[1], 127, 1)
        return [jnp.where(lane_f == 127, high, low), high]

    def shift_w(halves):
        low, high = pltpu.roll(halves[0], 1, 1), pltpu.roll(halves[1], 1, 1)
        return [low, jnp.where(lane_f == 0, low, high)]

    def north_step(ref, i):
        wet = [level < mask_row(h, 2, i) for h in range(2)]
        return [jnp.where(wet[h], at(ref, i + 1, h, t) - at(ref, i, h, t), 0.0) for t, h in places]

    def laplace(ref, first, last):
        def step(i, below):
            above = north_step(ref, i)
            wet = [level < mask_row(h, 1, i) for h in range(2)]
            for t in range(2):
                x = [at(ref, i, h, t) for h in range(2)]
                xe = shift_e(x)
                flux = []
                for h in range(2):
                    SX[i, h, 32 * t : 32 * t + 32, :] = x[h] + xe[h]
                    flux.append(jnp.where(wet[h], xe[h] - x[h], 0.0))
                flux_w = shift_w(flux)
                for h in range(2):
                    total = (flux[h] - flux_w[h]) + (above[2 * t + h] - below[2 * t + h])
                    LP[i, h, 32 * t : 32 * t + 32, :] = mixing * total
            return above

        row_pairs(first, last, step, north_step(ref, first - 1))

    def north_flux(ref, i):
        flux = []
        wet = [level < mask_row(h, 2, i) for h in range(2)]
        for t, h in places:
            value = V[i, 1, h] * (at(ref, i, h, t) + at(ref, i + 1, h, t))
            value += bare(LP, i + 1, h, t) - bare(LP, i, h, t)
            flux.append(jnp.where(wet[h], value, 0.0))
        return flux

    def tendency(ref, first, last, put):
        def step(i, below):
            above = north_flux(ref, i)
            wet_e = [level < mask_row(h, 1, i) for h in range(2)]
            deep = [mask_row(h, 0, i) for h in range(2)]
            wet_u = [level + 1.0 < deep[h] for h in range(2)]
            wet_d = [jnp.logical_and(level > 0.0, level < deep[h]) for h in range(2)]
            results = []
            for t in range(2):
                lap = [bare(LP, i, h, t) for h in range(2)]
                lape = shift_e(lap)
                flux = []
                for h in range(2):
                    value = V[i, 0, h] * bare(SX, i, h, t) + (lape[h] - lap[h])
                    flux.append(jnp.where(wet_e[h], value, 0.0))
                flux_w = shift_w(flux)
                for h in range(2):
                    x = at(ref, i, h, t)
                    up = jnp.where(wet_u[h], at(ref, i, h, t, 1) - x, 0.0)
                    down = jnp.where(wet_d[h], x - at(ref, i, h, t, -1), 0.0)
                    total = (flux_w[h] - flux[h]) + (below[2 * t + h] - above[2 * t + h])
                    results.append((x, total + lifting * (up - down)))
            put(i, results)
            return above

        row_pairs(first, last, step, north_flux(ref, first - 1))

    def put_middle(i, results):
        for (t, h), (x, half) in zip(places, results):
            M[i, h, 8 + 32 * t : 40 + 32 * t, :] = x + half

    def rim(value):
        return jnp.where(lane16 < 4, value, pltpu.roll(value, 120, 1))

    def patched(value, rims, q, h):
        pulled = pltpu.roll(rims, (124 - 16 * q) % 128, 1)
        return jnp.where(lane < 2, pulled, value) if h == 0 else jnp.where(lane >= 126, pulled, value)

    def patch_middle(i, carry):
        value = Ms[i]
        rims = rim(value)
        parts = []
        for q in range(8):
            pair = [patched(M[i, h, 8 * q + 8 : 8 * q + 16, :], rims, q, h) for h in range(2)]
            for h in range(2):
                M[i, h, 8 * q + 8 : 8 * q + 16, :] = pair[h]
            parts.append(tuple(pair))
        own = seam_of(parts)
        own = jnp.where(lane16 < 4, own, pltpu.roll(own, 8, 1))
        Ms[i] = jnp.where(jnp.logical_and(lane16 >= 4, lane16 < 12), value, own)
        return carry

    def put_updated(i, results):
        rims = rim(Xs[i])
        wet = [level < mask_row(h, 0, i) for h in range(2)]
        sums = [[], []]
        for (t, h), (m, half) in zip(places, results):
            value = 0.5 * ((at(X, i, h, t) + m) + half)
            value = jnp.concatenate(
                [patched(value[8 * g : 8 * g + 8], rims, 4 * t + g, h) for g in range(4)], axis=0
            )
            U[i - HALO, h, 32 * t : 32 * t + 32, :] = value
            part = jnp.where(wet[h], value, 0.0)
            sums[t].append((part[0:8] + part[8:16]) + (part[16:24] + part[24:32]))
        for h in range(2):
            FS[i - HALO, h] = sums[0][h] - 0.5 * sums[1][h]

    def seam_row(own, from_east, from_west, n):
        value = jnp.where(lane16 < 4, own, pltpu.roll(own, 8, 1))
        right = pltpu.roll(from_east, (4 - 4 * n) % 128, 1) if n != 1 else from_east
        left = pltpu.roll(from_west, (8 - 4 * n) % 128, 1) if n != 2 else from_west
        value = jnp.where(lane16 // 4 == 1, right, value)
        return jnp.where(lane16 // 4 == 2, left, value)

    def put_velocity(i, both):
        other = pltpu.roll(both, 64, 1)
        Us[i] = jnp.where(lane < 64, both, other)
        Vs[i] = jnp.where(lane < 64, other, both)

    level_s = (sub + 8 * lax.rem(laneq, 4)).astype(F32)

    def seam_masks(depth, rows):
        wide = iota(depth[0].shape, 1)
        seam_e = jnp.where(wide >= 124, depth[1], depth[2])
        seam_w = jnp.where(wide >= 124, depth[2], depth[0])
        base = jnp.where(wide < 8, pltpu.roll(seam_e, 4, 1), pltpu.roll(seam_w, 12, 1))
        base = jnp.where(wide < 16, base, 0.0)
        for turn in (16, 32, 64):
            base = base + pltpu.roll(base, turn, 1)
        deep = jnp.stack([jnp.broadcast_to(base[r : r + 1, :], (8, 128)) for r in rows], axis=0)
        wet_e = level_s[None] < jnp.minimum(deep, pltpu.roll(deep, 127, 2))
        wet_n = level_s[None] < jnp.minimum(deep[:-1], deep[1:])
        return wet_e, wet_n, level_s[None] + 1.0 < deep

    def seam_tendency(ref, first, last, masks):
        wet_e, wet_n, wet_u = masks
        x = ref[first - 2 : last + 2]
        xe = pltpu.roll(x, 127, 2)
        flux = jnp.where(wet_e, xe - x, 0.0)
        flux_n = jnp.where(wet_n, x[1:] - x[:-1], 0.0)
        lap = mixing * ((flux - pltpu.roll(flux, 1, 2))[1:-1] + (flux_n[1:] - flux_n[:-1]))
        x, xe = x[1:-1], xe[1:-1]
        flux = Us[first:last] * (x + xe)[1:-1] + (pltpu.roll(lap, 127, 2) - lap)[1:-1]
        flux = jnp.where(wet_e[2:-2], flux, 0.0)
        flux_n = Vs[first - 1 : last] * (x[1:] + x[:-1]) + (lap[1:] - lap[:-1])
        flux_n = jnp.where(wet_n[1:-1], flux_n, 0.0)
        x = x[1:-1]
        turned = pltpu.roll(x, 112, 2)
        upper = jnp.where(sub[None] < 7, pltpu.roll(x, 7, 1), pltpu.roll(turned, 7, 1))
        up = jnp.where(wet_u[2:-2], upper - x, 0.0)
        turned = pltpu.roll(up, 16, 2)
        down = jnp.where(sub[None] > 0, pltpu.roll(up, 1, 1), pltpu.roll(turned, 1, 1))
        total = (pltpu.roll(flux, 1, 2) - flux) + (flux_n[:-1] - flux_n[1:])
        return x, total + lifting * (up - down)

    def part_of(masks, first, last):
        return masks[0][first:last], masks[1][first : last - 1], masks[2][first:last]

    def seam_middle(first, last, masks):
        x, half = seam_tendency(Xs, first, last, masks)
        Ms[first:last] = x + half

    def seam_updated(first, last, masks):
        m, half = seam_tendency(Ms, first, last, masks)
        Xs[first:last] = 0.5 * ((Xs[first:last] + m) + half)

    laplace(X, 5, 19)
    tendency(X, 6, 18, put_middle)

    for copy in c_side:
        copy.wait()
    for a in range(4):
        for n in range(4):
            i = HALO + 4 * a + n
            Xs[i] = seam_row(Qt[4 * a + n], pack_in[1, 1 + 2 * a], pack_in[0, 1 + 2 * a], n)
            put_velocity(i, seam_row(Qv[4 * a + n], pack_in[1, 2 + 2 * a], pack_in[0, 2 + 2 * a], n))

    def beside(f, tile, right, left):
        j = 2 * f + tile
        right = pltpu.roll(right, 128 - 4 * j, 1) if j else right
        return jnp.where(lane < 64, right, pltpu.roll(left, 124 - 4 * j, 1))

    inside = [[jnp.concatenate([FL[h, tile, f] for tile in range(2)], axis=0) for h in range(2)] for f in range(2)]
    for f in range(2):
        inside[f].append(jnp.concatenate([beside(f, tile, pack_in[1, 0], pack_in[0, 0]) for tile in range(2)], axis=0))
    masks = seam_masks(inside[0], range(16))
    seam_middle(6, 18, masks)
    row_pairs(6, 18, patch_middle)
    seam_updated(8, 16, part_of(masks, 2, 14))
    laplace(M, 7, 17)
    tendency(M, 8, 16, put_updated)

    for copy in c_far:
        copy.wait()
    for j in range(3):
        X[j, :, 8:72, :] = xb_in[0, j].astype(F32)
        X[21 + j, :, 8:72, :] = xb_in[1, j].astype(F32)
    for j in range(2):
        V[2 + j] = vbn_in[1 + j].astype(F32)
        V[20 + j] = vbs_in[j].astype(F32)
    V[1, 1] = vbn_in[0, 1].astype(F32)

    rims = []
    for f in range(2):
        rim_f = []
        for h in range(2):
            from_north, from_south = ft_in[1, h], ft_in[0, h]
            if f == 0:
                rim_f.append(jnp.where(sub < 4, from_north, pltpu.roll(from_south, 4, 0)))
            else:
                rim_f.append(jnp.where(sub < 4, pltpu.roll(from_north, 4, 0), from_south))
        above = beside(f, 0, corner_in[3, 0], corner_in[1, 0])
        below = beside(f, 1, corner_in[2, 2], corner_in[0, 2])
        rim_f.append(jnp.where(sub < 4, above, below))
        rims.append(rim_f)
    no_north = (sub < 4).astype(jnp.int32) * (la == lats - 1).astype(jnp.int32)
    no_south = (sub >= 4).astype(jnp.int32) * (la == 0).astype(jnp.int32)
    outside = (no_north + no_south) > 0
    rims[0] = [jnp.where(outside, 0.0, p) for p in rims[0]]
    depth = [jnp.concatenate([inside[0][k], rims[0][k]], axis=0) for k in range(3)]
    diagonal = [6.0 + jnp.concatenate([inside[1][k], rims[1][k]], axis=0) for k in range(3)]
    put_masks(depth)

    for first in (1, 19):
        laplace(X, first, first + 4)
    for first in (2, 18):
        tendency(X, first, first + 4, put_middle)
    for n in range(4):
        Xs[n] = seam_row(seam_x(n), corner_in[2, 0], corner_in[0, 0], n)
        Xs[20 + n] = seam_row(seam_x(20 + n), corner_in[3, 1], corner_in[1, 1], n)
        if n > 0:
            put_velocity(n, seam_row(seam_v(n), corner_in[2, 1], corner_in[0, 1], n))
        if n < 2:
            put_velocity(20 + n, seam_row(seam_v(20 + n), corner_in[3, 2], corner_in[1, 2], n))
    masks_low = seam_masks(depth, list(range(20, 24)) + list(range(6)))
    masks_high = seam_masks(depth, range(10, 20))
    seam_middle(2, 6, part_of(masks_low, 0, 8))
    seam_middle(18, 22, part_of(masks_high, 2, 10))
    row_pairs(2, 6, patch_middle)
    row_pairs(18, 22, patch_middle)
    seam_updated(4, 8, part_of(masks_low, 2, 10))
    seam_updated(16, 20, part_of(masks_high, 0, 8))
    laplace(M, 3, 7)
    laplace(M, 17, 21)
    tendency(M, 4, 8, put_updated)
    tendency(M, 16, 20, put_updated)

    def forcing_rows(first, last, h):
        return jnp.sum(FS[first:last, h], axis=1) * (1.0 / math.sqrt(LEVELS))

    for h in range(2):
        for tile in range(2):
            FO[h, tile] = forcing_rows(8 * tile, 8 * tile + 8, h)
    c_forcing = [
        send(FO.at[1, 1], gc.at[0], 4, (north, east), s2, r2),
        send(FO.at[1, 0], gc.at[1], 5, (south, east), s2, r2),
        send(FO.at[0, 1], gc.at[2], 6, (north, west), s2, r2),
        send(FO.at[0, 0], gc.at[3], 7, (south, west), s2, r2),
        send(FO.at[:, 1], gs, 0, (north, lo), s2, r2),
        send(FO.at[:, 0], gn, 1, (south, lo), s2, r2),
    ]
    c_forcing += [
        send(FO.at[1], gw, 2, (la, east), s2, r2),
        send(FO.at[0], ge, 3, (la, west), s2, r2),
    ]


    def put_rows(i, carry):
        for h in range(2):
            tout[h, pl.ds(i, 64, stride=ROWS), :] = U[i, h]
        return carry

    def put_out(n, carry):
        rows = pl.ds(pl.multiple_of(128 * n, 128), 128)
        for h in range(2):
            out[rows, 128 * h : 128 * h + 128] = tout[h, rows, :]
        return carry

    row_pairs(0, ROWS, put_rows)
    lax.fori_loop(0, 8, put_out, 0)
    row = iota((24, 128), 0)
    surface = [p > 0.0 for p in depth]
    inverse = [jnp.where(surface[k], 1.0 / diagonal[k], 0.0) for k in range(3)]
    weight = [jnp.where(row < 16, diagonal[k], 0.0) for k in range(2)]
    for copy in c_forcing:
        copy.wait()
    forcing = flat(
        [[FO[h, tile] for tile in range(2)] for h in range(2)],
        [gn[h] for h in range(2)], [gs[h] for h in range(2)],
        [ge[tile] for tile in range(2)], [gw[tile] for tile in range(2)],
        gc[3], gc[2], gc[1], gc[0],
    )

    def apply_b(parts):
        columns = [to_north(p) + to_south(p) for p in parts]
        mixed = [p + 0.5 * c for p, c in zip(parts, columns)]
        e, w = to_east(mixed), to_west(mixed)
        return [inverse[k] * (columns[k] + e[k] + w[k]) for k in range(3)]

    basis = [[forcing[k] * inverse[k] for k in range(3)]]
    basis.append(apply_b(basis[0]))
    for j in range(2, ITERS + 1):
        image = apply_b(basis[j - 1])
        basis.append([2.0 * image[k] - basis[j - 2][k] for k in range(3)])

    def partial(left, right):
        total = left[0] * right[0] + left[1] * right[1]
        total = total[0:8] + total[8:16]
        return jnp.sum(total, axis=0, keepdims=True)

    rows = []
    for j in range(ITERS):
        weighted = [weight[k] * basis[j][k] for k in range(2)]
        rows.append(partial(weighted, basis[j]))
        rows.append(partial(weighted, basis[j + 1]))
    sums = jnp.sum(jnp.concatenate(rows, axis=0), axis=1, keepdims=True)
    sa[...] = jnp.sum(jnp.where(lane == sub, sums, 0.0), axis=0, keepdims=True)

    def gather(src, dst, me, size, partner, ss, rr):
        copies = []
        for k in range(1, size):
            copy = pltpu.make_async_remote_copy(
                src_ref=src, dst_ref=dst.at[me], send_sem=ss.at[k], recv_sem=rr.at[me],
                device_id=partner(k), device_id_type=MESH,
            )
            copy.start()
            copies.append(copy)
        dst[me] = src[...]
        for k in range(1, size):
            copies[k - 1].wait_send()
            other = lax.rem(me + k, size)
            pltpu.make_async_remote_copy(
                src_ref=src, dst_ref=dst.at[other], send_sem=ss.at[k], recv_sem=rr.at[other],
                device_id=partner(k), device_id_type=MESH,
            ).wait_recv()
        parts = [dst[k] for k in range(size)]
        while len(parts) > 1:
            parts = [parts[k] + parts[k + 1] for k in range(0, len(parts) - 1, 2)] + parts[len(parts) - len(parts) % 2 :]
        return parts[0]

    sb[...] = gather(sa, ra, me_a, size_a, partner_a, sas, sar)
    total = gather(sb, rb, me_b, size_b, partner_b, sbs, sbr)
    inner = [jnp.broadcast_to(total[:, k : k + 1], (1, 128)) for k in range(8)]
    c = inner[:2] + [2.0 * inner[k] - inner[k % 2] for k in range(2, 8)]

    def gram(i, j):
        return 0.5 * (c[i + j] + c[abs(i - j)])

    def ratio(top, bottom):
        good = jnp.logical_and(bottom > 0.0, top > 0.0)
        return jnp.where(good, top / jnp.where(good, bottom, 1.0), 0.0)

    zero = jnp.zeros_like(c[0])
    resid = [jnp.ones_like(zero)]
    direction = list(resid)
    pressure = [zero] * ITERS
    product = c[0]
    for k in range(ITERS):
        image = list(direction) + [zero]
        for j, value in enumerate(direction):
            if j == 0:
                image[1] = image[1] - value
            else:
                image[j + 1] = image[j + 1] - 0.5 * value
                image[j - 1] = image[j - 1] - 0.5 * value
        bottom = zero
        for i, value in enumerate(direction):
            line = zero
            for j, other in enumerate(image):
                line = line + other * gram(i, j)
            bottom = bottom + value * line
        alpha = ratio(product, bottom)
        for j, value in enumerate(direction):
            pressure[j] = pressure[j] + alpha * value
        if k + 1 < ITERS:
            resid = [a - alpha * b for a, b in zip(resid + [zero], image)]
            following = zero
            for i, value in enumerate(resid):
                line = zero
                for j, other in enumerate(resid):
                    line = line + other * gram(i, j)
                following = following + value * line
            beta = ratio(following, product)
            direction = [a + beta * b for a, b in zip(resid, direction + [zero])]
            product = following

    field = []
    for k in range(3):
        value = pressure[0] * basis[0][k]
        for j in range(1, ITERS):
            value = value + pressure[j] * basis[j][k]
        field.append(value)
    field_e = to_east(field)
    wet = [jnp.where(surface[k], 1.0, 0.0) for k in range(3)]
    wet_e = to_east(wet)
    for h in range(2):
        slope_e = wet[h] * wet_e[h] * (field_e[h] - field[h])
        slope_n = wet[h] * to_north(wet[h]) * (to_north(field[h]) - field[h])
        grad[0, :, 128 * h : 128 * h + 128] = slope_e[0:16]
        grad[1, :, 128 * h : 128 * h + 128] = slope_n[0:16]


def body(lats, lons, tracers, east_velocity, north_velocity, column_levels, surface_term):
    tall = 2 * LEVELS * ROWS
    cells = tracers.reshape(2 * LEVELS, ROWS, 256)
    east = east_velocity.reshape(LEVELS * ROWS, 256)
    north = north_velocity.reshape(LEVELS * ROWS, 256)
    size_a, size_b = lats // NZ, NZ * lons
    vmem = pltpu.VMEM
    scratch = [
        vmem((2, 2, LEVELS * ROWS, 128), BF16),
        vmem((2, 2, LEVELS * ROWS, 128), F32),
        vmem((ROWS, 256), jnp.int32),
        vmem((ROWS, 256), F32),
        vmem((HIGH, 2, 80, 128), F32),
        vmem((HIGH, 2, 80, 128), F32),
        vmem((HIGH, 2, 64, 128), F32),
        vmem((HIGH, 2, 64, 128), F32),
        vmem((HIGH, 2, 2, LEVELS, 128), F32),
        vmem((ROWS, 2, 64, 128), F32),
        vmem((HIGH, 8, 128), F32),
        vmem((HIGH, 8, 128), F32),
        vmem((HIGH, 8, 128), F32),
        vmem((HIGH, 8, 128), F32),
        vmem((ROWS, 8, 128), F32),
        vmem((ROWS, 8, 128), F32),
        vmem((2, 10, 8, 128), F32),
        vmem((2, 9, 8, 128), F32),
        vmem((4, 3, 8, 128), F32),
        vmem((2, 3, 2, 64, 128), BF16),
        vmem((2, 3, 2, 64, 128), BF16),
        vmem((3, 2, 2, LEVELS, 128), BF16),
        vmem((2, 2, 2, LEVELS, 128), BF16),
        vmem((3, 2, 2, LEVELS, 128), BF16),
        vmem((2, 2, 2, LEVELS, 128), BF16),
        vmem((2, 2, 2, 8, 128), F32),
        vmem((2, 2, 8, 128), F32),
        vmem((2, 2, 8, 128), F32),
        vmem((2, 2, 8, 128), F32),
        vmem((2, 8, 128), F32),
        vmem((2, 8, 128), F32),
        vmem((2, 8, 128), F32),
        vmem((2, 8, 128), F32),
        vmem((4, 8, 128), F32),
        vmem((2, 3, HIGH, 128), F32),
        vmem((ROWS, 2, 8, 128), F32),
        vmem((2, tall, 128), F32),
        vmem((1, 128), F32),
        vmem((size_a, 1, 128), F32),
        vmem((1, 128), F32),
        vmem((size_b, 1, 128), F32),
        pltpu.SemaphoreType.DMA((6 + 2 * ROWS,)),
        pltpu.SemaphoreType.DMA((15,)),
        pltpu.SemaphoreType.DMA((15,)),
        pltpu.SemaphoreType.DMA((8,)),
        pltpu.SemaphoreType.DMA((8,)),
        pltpu.SemaphoreType.DMA((size_a,)),
        pltpu.SemaphoreType.DMA((size_a,)),
        pltpu.SemaphoreType.DMA((size_b,)),
        pltpu.SemaphoreType.DMA((size_b,)),
    ]
    hbm, near = pl.BlockSpec(memory_space=pltpu.HBM), pl.BlockSpec(memory_space=pltpu.VMEM)
    updated, gradient = pl.pallas_call(
        functools.partial(kernel, lats, lons),
        out_shape=(pltpu.VMEM((tall, 256), F32), pltpu.VMEM((2, ROWS, 256), F32)),
        in_specs=[hbm] * 5,
        out_specs=(near, near),
        scratch_shapes=scratch,
        compiler_params=pltpu.CompilerParams(
            collective_id=0, has_side_effects=True, vmem_limit_bytes=40 * 1024 * 1024
        ),
    )(*[pltpu.with_memory_space_constraint(x, pltpu.HBM) for x in (cells, east, north, column_levels, surface_term)])
    return updated.reshape(2, LEVELS, ROWS, 256), gradient


def solution(mesh):
    in_specs = (
        P(None, None, "lat", "lon"),
        P(None, "lat", "lon"),
        P(None, "lat", "lon"),
        P("lat", "lon"),
        P("lat", "lon"),
    )
    out_specs = (P(None, None, "lat", "lon"), P(None, "lat", "lon"))
    step = functools.partial(body, mesh.shape["lat"], mesh.shape["lon"])
    return jax.shard_map(step, mesh=mesh, in_specs=in_specs, out_specs=out_specs, check_vma=False)
```

```python
import functools
import math

import jax
import jax.numpy as jnp
from jax import lax
from jax.experimental import pallas as pl
from jax.experimental.pallas import tpu as pltpu
from jax.sharding import PartitionSpec as P

MESH = pl.DeviceIdType.MESH
F32 = jnp.float32
BF16 = jnp.bfloat16

ITERS = 4
LEVELS = 32
ROWS = 16
HALO = 4
HIGH = ROWS + 2 * HALO
NX = 4
NZ = 2

time_step = 0.5
biharm_coef = 0.05
vertical_coef = 0.8


def iota(shape, axis):
    return lax.broadcasted_iota(jnp.int32, shape, axis)


def kernel(
    lats, lons, trc, vel_e, vel_n, levels_in, term_in, out, grad,
    vin, vf, levi, termi, X, M, LP, SX, GC, V, U, Xs, Ms, Us, Vs, Qt, Qv, pack, pack_in, corner_in,
    xb, xb_in, vbn, vbs, vbn_in, vbs_in, FL, FT, ft_in,
    FO, gn, gs, ge, gw, gc, MK, FS, tout, sa, ra, sb, rb,
    in_sem, s1, r1, s2, r2, sas, sar, sbs, sbr,
):
    la, lo = lax.axis_index("lat"), lax.axis_index("lon")
    north, south = lax.rem(la + 1, lats), lax.rem(la + lats - 1, lats)
    east, west = lax.rem(lo + 1, lons), lax.rem(lo + lons - 1, lons)
    ny = lats // (NX * NZ)
    y, zx = la // (NX * NZ), lax.rem(la, NX * NZ)
    zz, xx = zx // NX, lax.rem(zx, NX)
    size_a, size_b = ny * NX, NZ * lons
    me_a, me_b = y * NX + xx, zz * lons + lo

    def turns(value, count):
        return [value] + [jnp.where(value + d >= count, value + d - count, value + d) for d in range(1, count)]

    xs, ys, zs, ls = turns(xx, NX), turns(y, ny), turns(zz, NZ), turns(lo, lons)

    def partner_a(k):
        y_k, x_k = ys[k // NX], xs[k % NX]
        return ((y_k * NZ + zz) * NX + x_k, lo), y_k * NX + x_k

    def partner_b(k):
        z_k, l_k = zs[k // lons], ls[k % lons]
        return ((y * NZ + z_k) * NX + xx, l_k), z_k * lons + l_k

    barrier = pltpu.get_barrier_semaphore()
    around = [
        (north, east), (south, east), (north, west), (south, west),
        (north, lo), (south, lo), (la, east), (la, west),
    ]
    def ring(d, count):
        return min(d, count - d)

    far_a = sorted(range(1, size_a), key=lambda k: -ring(k // NX, ny) - ring(k % NX, NX))
    far_b = sorted(range(1, size_b), key=lambda k: -ring(k % lons, lons) - 0.5 * (k // lons))
    partners = [partner_a(k)[0] for k in far_a] + [partner_b(k)[0] for k in far_b]

    def greet(devices):
        for device in devices:
            pl.semaphore_signal(barrier, inc=1, device_id=device, device_id_type=MESH)

    greet(around)

    loads = [
        pltpu.make_async_copy(levels_in, levi, in_sem.at[0]),
        pltpu.make_async_copy(term_in, termi, in_sem.at[1]),
    ]
    edge_rows = [0, 1, 2, 3, 12, 13, 14, 15]
    inner_rows = list(range(4, 12))

    def load_rows(rows):
        return [
            pltpu.make_async_copy(
                trc.at[:, r, pl.ds(128 * h, 128)], X.at[r + HALO, h, pl.ds(8, 64)], in_sem.at[6 + 2 * r + h]
            )
            for r in rows
            for h in range(2)
        ]

    x_loads = load_rows(edge_rows)
    v_loads = [
        pltpu.make_async_copy(src.at[:, pl.ds(128 * h, 128)], vin.at[w, h], in_sem.at[2 + 2 * w + h])
        for w, src in enumerate((vel_e, vel_n))
        for h in range(2)
    ]
    y_loads = load_rows(inner_rows)
    for load in loads + x_loads + v_loads + y_loads:
        load.start()
    greet(partners)

    def send(src, dst, k, device, ss=s1, rr=r1):
        copy = pltpu.make_async_remote_copy(
            src_ref=src, dst_ref=dst, send_sem=ss.at[k], recv_sem=rr.at[k], device_id=device, device_id_type=MESH
        )
        copy.start()
        return copy

    lane = iota((8, 128), 1)
    sub = iota((8, 128), 0)
    lane16 = lax.rem(lane, 16)
    laneq = lane // 16

    def rows_of(first, last, step, carry=0, size=2):
        def group(n, carry):
            for r in range(size):
                carry = step(first + size * n + r, carry)
            return carry

        return lax.fori_loop(0, (last - first) // size, group, carry)

    for load in loads:
        load.wait()
    for h in range(2):
        for tile in range(2):
            FL[h, tile, 0] = levi[8 * tile : 8 * tile + 8, 128 * h : 128 * h + 128].astype(F32)
            FL[h, tile, 1] = termi[8 * tile : 8 * tile + 8, 128 * h : 128 * h + 128]

    for h in range(2):
        FT[0, h] = jnp.where(sub < 4, pltpu.roll(FL[h, 1, 0], 4, 0), FL[h, 1, 1])
        FT[1, h] = jnp.where(sub < 4, FL[h, 0, 0], pltpu.roll(FL[h, 0, 1], 4, 0))
    for side in range(2):
        packed = jnp.zeros((8, 128), F32)
        for f in range(2):
            for tile in range(2):
                j = 2 * f + tile
                turn = (4 * j + 4) % 128 if side == 0 else 4 * j
                value = FL[1 - side, tile, f]
                packed = jnp.where(lane // 4 == j, pltpu.roll(value, turn, 1) if turn else value, packed)
        pack[side, 0] = packed
        pack[side, 9] = packed

    for load in x_loads:
        load.wait()
    for j in range(3):
        xb[0, j] = X[16 + j, :, 8:72, :].astype(BF16)
        xb[1, j] = X[5 + j, :, 8:72, :].astype(BF16)

    for load in v_loads:
        load.wait()

    def widen(n, carry):
        rows = pl.ds(pl.multiple_of(64 * n, 64), 64)
        for w in range(2):
            for h in range(2):
                vf[w, h, rows, :] = vin[w, h, rows, :].astype(F32) * (0.5 * time_step)
        return carry

    lax.fori_loop(0, 8, widen, 0)

    def fill_v(i, carry):
        for w in range(2):
            for h in range(2):
                V[i, w, h] = vf[w, h, pl.ds(i - HALO, 32, stride=ROWS), :]
        return carry

    rows_of(HALO, HALO + ROWS, fill_v, size=4)
    for j in range(3):
        vbn[j] = V[17 + j].astype(BF16)
    for j in range(2):
        vbs[j] = V[4 + j].astype(BF16)

    def seam_of(parts):
        out = jnp.zeros((8, 128), F32)
        for q, (low, high) in enumerate(parts):
            both = jnp.where(lane >= 124, high, low)
            out = jnp.where(laneq == q, pltpu.roll(both, (16 * q + 4) % 128, 1), out)
        return out

    def seam_x(i):
        return seam_of([(X[i, 0, 8 * q + 8 : 8 * q + 16, :], X[i, 1, 8 * q + 8 : 8 * q + 16, :]) for q in range(8)])

    def seam_v(i):
        return seam_of(
            [
                (V[i, q // 4, 0, 8 * (q % 4) : 8 * (q % 4) + 8, :], V[i, q // 4, 1, 8 * (q % 4) : 8 * (q % 4) + 8, :])
                for q in range(8)
            ]
        )

    def pack_rows(i, carry):
        Qt[i - HALO] = seam_x(i)
        Qv[i - HALO] = seam_v(i)
        return carry

    for load in y_loads:
        load.wait()
    rows_of(HALO, HALO + ROWS, pack_rows, size=8)
    for a in range(4):
        for w, Q in enumerate((Qt, Qv)):
            for side in range(2):
                packed = jnp.zeros((8, 128), F32)
                for n in range(4):
                    turn = (4 * n - 4 * side) % 128
                    value = Q[4 * a + n]
                    packed = jnp.where(lane16 // 4 == n, pltpu.roll(value, turn, 1) if turn else value, packed)
                pack[side, 1 + 2 * a + w] = packed

    pl.semaphore_wait(barrier, len(around) + len(partners))

    body_rows = pl.ds(8, 64)
    c_side = [
        send(pack.at[0, pl.ds(0, 9)], pack_in.at[0], 0, (la, east)),
        send(pack.at[1, pl.ds(0, 9)], pack_in.at[1], 1, (la, west)),
    ]
    c_far = [
        send(pack.at[0, pl.ds(7, 3)], corner_in.at[0], 2, (north, east)),
        send(pack.at[0, pl.ds(0, 3)], corner_in.at[1], 3, (south, east)),
        send(pack.at[1, pl.ds(7, 3)], corner_in.at[2], 4, (north, west)),
        send(pack.at[1, pl.ds(0, 3)], corner_in.at[3], 5, (south, west)),
        send(FT.at[0], ft_in.at[0], 6, (north, lo)),
        send(FT.at[1], ft_in.at[1], 7, (south, lo)),
        send(X.at[19, :, body_rows], X.at[3, :, body_rows], 8, (north, lo)),
        send(X.at[4, :, body_rows], X.at[20, :, body_rows], 9, (south, lo)),
        send(xb.at[0], xb_in.at[0], 10, (north, lo)),
        send(xb.at[1], xb_in.at[1], 11, (south, lo)),
        send(vbn.at[pl.ds(1, 2)], vbn_in.at[pl.ds(1, 2)], 12, (north, lo)),
        send(vbn.at[0, 1], vbn_in.at[0, 1], 13, (north, lo)),
        send(vbs, vbs_in, 14, (south, lo)),
    ]

    def flat(own, n, s, e, w, ne, se, nw, sw):
        parts = [jnp.concatenate([own[h][0], own[h][1], jnp.where(sub < 4, n[h], s[h])], axis=0) for h in range(2)]
        right = jnp.concatenate([e[0], e[1], jnp.where(sub < 4, ne, se)], axis=0)
        left = jnp.concatenate([w[0], w[1], jnp.where(sub < 4, nw, sw)], axis=0)
        parts.append(jnp.where(iota((24, 128), 1) < 64, right, left))
        return parts

    def to_east(parts):
        rolled = [pltpu.roll(p, 127, 1) for p in parts]
        last = iota(parts[0].shape, 1) == 127
        return [jnp.where(last, rolled[(k + 1) % 3], rolled[k]) for k in range(3)]

    def to_west(parts):
        rolled = [pltpu.roll(p, 1, 1) for p in parts]
        first = iota(parts[0].shape, 1) == 0
        return [jnp.where(first, rolled[(k + 2) % 3], rolled[k]) for k in range(3)]

    def to_north(part):
        return pltpu.roll(part, 23, 0)

    def to_south(part):
        return pltpu.roll(part, 1, 0)

    def put_masks(depth):
        east_depth = to_east(depth)
        for h in range(2):
            MK[h, 0] = depth[h]
            MK[h, 1] = jnp.minimum(depth[h], east_depth[h])
            MK[h, 2] = jnp.minimum(depth[h], to_north(depth[h]))

    dry = jnp.zeros((8, 128), F32)
    put_masks([jnp.concatenate([FL[h, 0, 0], FL[h, 1, 0], dry], axis=0) for h in range(2)] + [jnp.zeros((24, 128), F32)])

    level = sub.astype(F32)
    mixing = time_step * biharm_coef
    lifting = time_step * vertical_coef

    def mask_row(h, n, i):
        return MK[h, n, pl.ds(jnp.where(i >= HALO, i - HALO, i + 20), 1), :]

    def at(ref, i, h, t, g, up=0):
        start = 8 + 32 * t + 8 * g + up
        return ref[i, h, start : start + 8, :]

    def bare(t, g):
        return slice(32 * t + 8 * g, 32 * t + 8 * g + 8)

    def shift_e(halves):
        low, high = pltpu.roll(halves[0], 127, 1), pltpu.roll(halves[1], 127, 1)
        return [jnp.where(lane == 127, high, low), high]

    def shift_w(halves):
        low, high = pltpu.roll(halves[0], 1, 1), pltpu.roll(halves[1], 1, 1)
        return [low, jnp.where(lane == 0, low, high)]

    def pull(rims, q):
        return None if rims is None else pltpu.roll(rims, (124 - 16 * q) % 128, 1)

    def laplace(ref, firsts, count, size=2):
        def group(ref, i):
            edge_e = [[mask_row(h, 1, i + r) for h in range(2)] for r in range(size)]
            edge_n = [[mask_row(h, 2, i + r) for h in range(2)] for r in range(-1, size)]
            for g in range(4):
                here = level + 8.0 * g
                wet_e = [[here < edge for edge in pair] for pair in edge_e]
                wet_n = [[here < edge for edge in pair] for pair in edge_n]
                for t in range(2):
                    x = [[at(ref, i + r, h, t, g) for h in range(2)] for r in range(-1, size + 1)]
                    north_flux = [
                        [jnp.where(wet_n[r][h], x[r + 1][h] - x[r][h], 0.0) for h in range(2)]
                        for r in range(size + 1)
                    ]
                    for r in range(size):
                        mid = x[r + 1]
                        xe = shift_e(mid)
                        flux = [jnp.where(wet_e[r][h], xe[h] - mid[h], 0.0) for h in range(2)]
                        flux_w = shift_w(flux)
                        for h in range(2):
                            SX[i + r, h, bare(t, g), :] = mid[h] + xe[h]
                            total = (flux[h] - flux_w[h]) + (north_flux[r + 1][h] - north_flux[r][h])
                            LP[i + r, h, bare(t, g), :] = mixing * total

        def step(n, carry):
            for first in firsts:
                group(ref, first + size * n)
            return carry

        lax.fori_loop(0, count // size, step, 0)

    def northward(ref, i, wet, x, xn, lap, lapn, h, g):
        value = V[i, 1, h, 8 * g : 8 * g + 8, :] * (x + xn) + (lapn - lap)
        return jnp.where(wet, value, 0.0)

    def tendency(ref, firsts, count, put, finish, begin=lambda i: None, size=2):
        for block, first in enumerate(firsts):
            edge = [mask_row(h, 2, first - 1) for h in range(2)]
            for g in range(4):
                for t in range(2):
                    for h in range(2):
                        GC[block, h, bare(t, g), :] = northward(
                            ref, first - 1, level + 8.0 * g < edge[h],
                            at(ref, first - 1, h, t, g), at(ref, first, h, t, g),
                            LP[first - 1, h, bare(t, g), :], LP[first, h, bare(t, g), :], h, g,
                        )

        def group(block, i):
            deep, edge_e, edge_n = [
                [[mask_row(h, k, i + r) for h in range(2)] for r in range(size)] for k in range(3)
            ]
            done = [[None, None] for _ in range(size)]
            rims = [begin(i + r) for r in range(size)]
            for g in range(4):
                here = level + 8.0 * g
                for t in range(2):
                    x = [[at(ref, i + r, h, t, g) for h in range(2)] for r in range(size + 1)]
                    lap = [[LP[i + r, h, bare(t, g), :] for h in range(2)] for r in range(size + 1)]
                    below = [GC[block, h, bare(t, g), :] for h in range(2)]
                    for r in range(size):
                        pulled = pull(rims[r], 4 * t + g)
                        lape = shift_e(lap[r])
                        flux = []
                        for h in range(2):
                            value = V[i + r, 0, h, 8 * g : 8 * g + 8, :] * SX[i + r, h, bare(t, g), :]
                            value += lape[h] - lap[r][h]
                            flux.append(jnp.where(here < edge_e[r][h], value, 0.0))
                        flux_w = shift_w(flux)
                        for h in range(2):
                            mid = x[r][h]
                            above = northward(
                                ref, i + r, here < edge_n[r][h], mid, x[r + 1][h], lap[r][h], lap[r + 1][h], h, g
                            )
                            total = (flux_w[h] - flux[h]) + (below[h] - above)
                            below[h] = above
                            up = jnp.where(here + 1.0 < deep[r][h], at(ref, i + r, h, t, g, 1) - mid, 0.0)
                            wet_d = here < deep[r][h]
                            if g == 0:
                                wet_d = jnp.logical_and(wet_d, sub > 0)
                            down = jnp.where(wet_d, mid - at(ref, i + r, h, t, g, -1), 0.0)
                            part = put(i + r, t, g, h, mid, total + lifting * (up - down), deep[r][h], pulled)
                            if part is not None:
                                done[r][h] = part if done[r][h] is None else done[r][h] + part
                    for h in range(2):
                        GC[block, h, bare(t, g), :] = below[h]
            for r in range(size):
                finish(i + r, done[r])

        def step(n, carry):
            for block, first in enumerate(firsts):
                group(block, first + size * n)
            return carry

        lax.fori_loop(0, count // size, step, 0)

    def put_middle(i, t, g, h, x, half, deep, pulled):
        M[i, h, 8 + 32 * t + 8 * g : 16 + 32 * t + 8 * g, :] = x + half

    def nothing(i, done):
        pass

    def rim(value):
        return jnp.where(lane16 < 4, value, pltpu.roll(value, 120, 1))

    def patched(value, pulled, h):
        return jnp.where(lane < 2, pulled, value) if h == 0 else jnp.where(lane >= 126, pulled, value)

    def patch_middle(i, carry):
        value = Ms[i]
        rims = rim(value)
        parts = []
        for q in range(8):
            pulled = pull(rims, q)
            pair = [patched(M[i, h, 8 * q + 8 : 8 * q + 16, :], pulled, h) for h in range(2)]
            for h in range(2):
                M[i, h, 8 * q + 8 : 8 * q + 16, :] = pair[h]
            parts.append(tuple(pair))
        own = seam_of(parts)
        own = jnp.where(lane16 < 4, own, pltpu.roll(own, 8, 1))
        Ms[i] = jnp.where(jnp.logical_and(lane16 >= 4, lane16 < 12), value, own)
        return carry

    def put_updated(i, t, g, h, m, half, deep, pulled):
        value = patched(0.5 * ((at(X, i, h, t, g) + m) + half), pulled, h)
        U[i - HALO, h, bare(t, g), :] = value
        part = jnp.where(level + 8.0 * g < deep, value, 0.0)
        return part if t == 0 else -0.5 * part

    def put_forcing(i, done):
        for h in range(2):
            FS[i - HALO, h] = done[h]

    def seam_row(own, from_east, from_west, n):
        value = jnp.where(lane16 < 4, own, pltpu.roll(own, 8, 1))
        right = pltpu.roll(from_east, (4 - 4 * n) % 128, 1) if n != 1 else from_east
        left = pltpu.roll(from_west, (8 - 4 * n) % 128, 1) if n != 2 else from_west
        value = jnp.where(lane16 // 4 == 1, right, value)
        return jnp.where(lane16 // 4 == 2, left, value)

    def put_velocity(i, both):
        other = pltpu.roll(both, 64, 1)
        Us[i] = jnp.where(lane < 64, both, other)
        Vs[i] = jnp.where(lane < 64, other, both)

    level_s = (sub + 8 * lax.rem(laneq, 4)).astype(F32)

    def seam_masks(depth, rows):
        wide = iota(depth[0].shape, 1)
        seam_e = jnp.where(wide >= 124, depth[1], depth[2])
        seam_w = jnp.where(wide >= 124, depth[2], depth[0])
        base = jnp.where(wide < 8, pltpu.roll(seam_e, 4, 1), pltpu.roll(seam_w, 12, 1))
        base = jnp.where(wide < 16, base, 0.0)
        for turn in (16, 32, 64):
            base = base + pltpu.roll(base, turn, 1)
        deep = jnp.stack([jnp.broadcast_to(base[r : r + 1, :], (8, 128)) for r in rows], axis=0)
        wet_e = level_s[None] < jnp.minimum(deep, pltpu.roll(deep, 127, 2))
        wet_n = level_s[None] < jnp.minimum(deep[:-1], deep[1:])
        return wet_e, wet_n, level_s[None] + 1.0 < deep

    def seam_tendency(ref, first, last, masks):
        wet_e, wet_n, wet_u = masks
        x = ref[first - 2 : last + 2]
        xe = pltpu.roll(x, 127, 2)
        flux = jnp.where(wet_e, xe - x, 0.0)
        flux_n = jnp.where(wet_n, x[1:] - x[:-1], 0.0)
        lap = mixing * ((flux - pltpu.roll(flux, 1, 2))[1:-1] + (flux_n[1:] - flux_n[:-1]))
        x, xe = x[1:-1], xe[1:-1]
        flux = Us[first:last] * (x + xe)[1:-1] + (pltpu.roll(lap, 127, 2) - lap)[1:-1]
        flux = jnp.where(wet_e[2:-2], flux, 0.0)
        flux_n = Vs[first - 1 : last] * (x[1:] + x[:-1]) + (lap[1:] - lap[:-1])
        flux_n = jnp.where(wet_n[1:-1], flux_n, 0.0)
        x = x[1:-1]
        turned = pltpu.roll(x, 112, 2)
        upper = jnp.where(sub[None] < 7, pltpu.roll(x, 7, 1), pltpu.roll(turned, 7, 1))
        up = jnp.where(wet_u[2:-2], upper - x, 0.0)
        turned = pltpu.roll(up, 16, 2)
        down = jnp.where(sub[None] > 0, pltpu.roll(up, 1, 1), pltpu.roll(turned, 1, 1))
        total = (pltpu.roll(flux, 1, 2) - flux) + (flux_n[:-1] - flux_n[1:])
        return x, total + lifting * (up - down)

    def part_of(masks, first, last):
        return masks[0][first:last], masks[1][first : last - 1], masks[2][first:last]

    def seam_middle(first, last, masks):
        x, half = seam_tendency(Xs, first, last, masks)
        Ms[first:last] = x + half

    def seam_updated(first, last, masks):
        m, half = seam_tendency(Ms, first, last, masks)
        Xs[first:last] = 0.5 * ((Xs[first:last] + m) + half)

    laplace(X, [5], 14)
    tendency(X, [6], 12, put_middle, nothing)

    for copy in c_side:
        copy.wait()
    for a in range(4):
        for n in range(4):
            i = HALO + 4 * a + n
            Xs[i] = seam_row(Qt[4 * a + n], pack_in[1, 1 + 2 * a], pack_in[0, 1 + 2 * a], n)
            put_velocity(i, seam_row(Qv[4 * a + n], pack_in[1, 2 + 2 * a], pack_in[0, 2 + 2 * a], n))

    def beside(f, tile, right, left):
        j = 2 * f + tile
        right = pltpu.roll(right, 128 - 4 * j, 1) if j else right
        return jnp.where(lane < 64, right, pltpu.roll(left, 124 - 4 * j, 1))

    inside = [[jnp.concatenate([FL[h, tile, f] for tile in range(2)], axis=0) for h in range(2)] for f in range(2)]
    for f in range(2):
        inside[f].append(jnp.concatenate([beside(f, tile, pack_in[1, 0], pack_in[0, 0]) for tile in range(2)], axis=0))
    masks = seam_masks(inside[0], range(16))
    seam_middle(6, 18, masks)
    rows_of(6, 18, patch_middle, size=6)
    seam_updated(8, 16, part_of(masks, 2, 14))
    laplace(M, [7], 10)
    tendency(M, [8], 8, put_updated, put_forcing, lambda i: rim(Xs[i]))

    for copy in c_far[4:6]:
        copy.wait()
    no_north = (sub < 4).astype(jnp.int32) * (la == lats - 1).astype(jnp.int32)
    no_south = (sub >= 4).astype(jnp.int32) * (la == 0).astype(jnp.int32)
    outside = (no_north + no_south) > 0
    rims = [[], []]
    for h in range(2):
        from_north, from_south = ft_in[1, h], ft_in[0, h]
        rims[0].append(jnp.where(outside, 0.0, jnp.where(sub < 4, from_north, pltpu.roll(from_south, 4, 0))))
        rims[1].append(jnp.where(sub < 4, pltpu.roll(from_north, 4, 0), from_south))
    depth = [jnp.concatenate([inside[0][h], rims[0][h]], axis=0) for h in range(2)]
    put_masks(depth + [jnp.zeros((24, 128), F32)])
    for copy in c_far[6:10]:
        copy.wait()
    for j in range(3):
        X[j, :, 8:72, :] = xb_in[0, j].astype(F32)
        X[21 + j, :, 8:72, :] = xb_in[1, j].astype(F32)
    laplace(X, [1, 19], 4)
    for copy in c_far[10:]:
        copy.wait()
    for j in range(2):
        V[2 + j] = vbn_in[1 + j].astype(F32)
        V[20 + j] = vbs_in[j].astype(F32)
    V[1, 1] = vbn_in[0, 1].astype(F32)
    tendency(X, [2, 18], 4, put_middle, nothing)

    for copy in c_far[:4]:
        copy.wait()
    for f in range(2):
        above = beside(f, 0, corner_in[3, 0], corner_in[1, 0])
        below = beside(f, 1, corner_in[2, 2], corner_in[0, 2])
        rims[f].append(jnp.where(sub < 4, above, below))
    rims[0][2] = jnp.where(outside, 0.0, rims[0][2])
    depth.append(jnp.concatenate([inside[0][2], rims[0][2]], axis=0))
    diagonal = [6.0 + jnp.concatenate([inside[1][k], rims[1][k]], axis=0) for k in range(3)]
    for n in range(4):
        Xs[n] = seam_row(seam_x(n), corner_in[2, 0], corner_in[0, 0], n)
        Xs[20 + n] = seam_row(seam_x(20 + n), corner_in[3, 1], corner_in[1, 1], n)
    for n in range(1, 4):
        put_velocity(n, seam_row(seam_v(n), corner_in[2, 1], corner_in[0, 1], n))
    for n in range(2):
        put_velocity(20 + n, seam_row(seam_v(20 + n), corner_in[3, 2], corner_in[1, 2], n))
    masks_low = seam_masks(depth, list(range(20, 24)) + list(range(6)))
    masks_high = seam_masks(depth, range(10, 20))
    seam_middle(2, 6, part_of(masks_low, 0, 8))
    seam_middle(18, 22, part_of(masks_high, 2, 10))
    for first in (2, 18):
        for r in range(4):
            patch_middle(first + r, 0)
    seam_updated(4, 8, part_of(masks_low, 2, 10))
    seam_updated(16, 20, part_of(masks_high, 0, 8))
    laplace(M, [3, 17], 4)
    tendency(M, [4, 16], 4, put_updated, put_forcing, lambda i: rim(Xs[i]))

    def forcing_rows(first, last, h):
        return jnp.sum(FS[first:last, h], axis=1) * (1.0 / math.sqrt(LEVELS))

    for h in range(2):
        for tile in range(2):
            FO[h, tile] = forcing_rows(8 * tile, 8 * tile + 8, h)
    c_forcing = [
        send(FO.at[1, 1], gc.at[0], 4, (north, east), s2, r2),
        send(FO.at[1, 0], gc.at[1], 5, (south, east), s2, r2),
        send(FO.at[0, 1], gc.at[2], 6, (north, west), s2, r2),
        send(FO.at[0, 0], gc.at[3], 7, (south, west), s2, r2),
        send(FO.at[:, 1], gs, 0, (north, lo), s2, r2),
        send(FO.at[:, 0], gn, 1, (south, lo), s2, r2),
    ]
    c_forcing += [
        send(FO.at[1], gw, 2, (la, east), s2, r2),
        send(FO.at[0], ge, 3, (la, west), s2, r2),
    ]


    def put_rows(i, carry):
        for h in range(2):
            tout[h, pl.ds(i, 64, stride=ROWS), :] = U[i, h]
        return carry

    def put_out(n, carry):
        rows = pl.ds(pl.multiple_of(128 * n, 128), 128)
        for h in range(2):
            out[rows, 128 * h : 128 * h + 128] = tout[h, rows, :]
        return carry

    rows_of(0, ROWS, put_rows)
    lax.fori_loop(0, 8, put_out, 0)
    row = iota((24, 128), 0)
    surface = [p > 0.0 for p in depth]
    inverse = [jnp.where(surface[k], 1.0 / diagonal[k], 0.0) for k in range(3)]
    weight = [jnp.where(row < 16, diagonal[k], 0.0) for k in range(2)]
    for copy in c_forcing:
        copy.wait()
    forcing = flat(
        [[FO[h, tile] for tile in range(2)] for h in range(2)],
        [gn[h] for h in range(2)], [gs[h] for h in range(2)],
        [ge[tile] for tile in range(2)], [gw[tile] for tile in range(2)],
        gc[3], gc[2], gc[1], gc[0],
    )

    def apply_b(parts):
        columns = [to_north(p) + to_south(p) for p in parts]
        mixed = [p + 0.5 * c for p, c in zip(parts, columns)]
        e, w = to_east(mixed), to_west(mixed)
        return [inverse[k] * (columns[k] + e[k] + w[k]) for k in range(3)]

    basis = [[forcing[k] * inverse[k] for k in range(3)]]
    basis.append(apply_b(basis[0]))
    for j in range(2, ITERS + 1):
        image = apply_b(basis[j - 1])
        basis.append([2.0 * image[k] - basis[j - 2][k] for k in range(3)])

    def partial(left, right):
        total = left[0] * right[0] + left[1] * right[1]
        total = total[0:8] + total[8:16]
        return jnp.sum(total, axis=0, keepdims=True)

    rows = []
    for j in range(ITERS):
        weighted = [weight[k] * basis[j][k] for k in range(2)]
        rows.append(partial(weighted, basis[j]))
        rows.append(partial(weighted, basis[j + 1]))
    sums = jnp.sum(jnp.concatenate(rows, axis=0), axis=1, keepdims=True)
    sa[...] = jnp.sum(jnp.where(lane == sub, sums, 0.0), axis=0, keepdims=True)

    def gather(src, dst, me, size, order, partner, ss, rr):
        copies = []
        for k in order:
            device, place = partner(k)
            copy = pltpu.make_async_remote_copy(
                src_ref=src, dst_ref=dst.at[me], send_sem=ss.at[k], recv_sem=rr.at[me],
                device_id=device, device_id_type=MESH,
            )
            copy.start()
            arrival = pltpu.make_async_remote_copy(
                src_ref=src, dst_ref=dst.at[place], send_sem=ss.at[k], recv_sem=rr.at[place],
                device_id=device, device_id_type=MESH,
            )
            copies.append((copy, arrival))
        dst[me] = src[...]
        for copy, arrival in copies:
            copy.wait_send()
            arrival.wait_recv()
        parts = [dst[k] for k in range(size)]
        while len(parts) > 1:
            parts = [parts[k] + parts[k + 1] for k in range(0, len(parts) - 1, 2)] + parts[len(parts) - len(parts) % 2 :]
        return parts[0]

    sb[...] = gather(sa, ra, me_a, size_a, far_a, partner_a, sas, sar)
    total = gather(sb, rb, me_b, size_b, far_b, partner_b, sbs, sbr)
    inner = [jnp.broadcast_to(total[:, k : k + 1], (1, 128)) for k in range(8)]
    c = inner[:2] + [2.0 * inner[k] - inner[k % 2] for k in range(2, 8)]

    def gram(i, j):
        return 0.5 * (c[i + j] + c[abs(i - j)])

    def ratio(top, bottom):
        good = jnp.logical_and(bottom > 0.0, top > 0.0)
        return jnp.where(good, top / jnp.where(good, bottom, 1.0), 0.0)

    zero = jnp.zeros_like(c[0])
    resid = [jnp.ones_like(zero)]
    direction = list(resid)
    pressure = [zero] * ITERS
    product = c[0]
    for k in range(ITERS):
        image = list(direction) + [zero]
        for j, value in enumerate(direction):
            if j == 0:
                image[1] = image[1] - value
            else:
                image[j + 1] = image[j + 1] - 0.5 * value
                image[j - 1] = image[j - 1] - 0.5 * value
        bottom = zero
        for i, value in enumerate(direction):
            line = zero
            for j, other in enumerate(image):
                line = line + other * gram(i, j)
            bottom = bottom + value * line
        alpha = ratio(product, bottom)
        for j, value in enumerate(direction):
            pressure[j] = pressure[j] + alpha * value
        if k + 1 < ITERS:
            resid = [a - alpha * b for a, b in zip(resid + [zero], image)]
            following = zero
            for i, value in enumerate(resid):
                line = zero
                for j, other in enumerate(resid):
                    line = line + other * gram(i, j)
                following = following + value * line
            beta = ratio(following, product)
            direction = [a + beta * b for a, b in zip(resid, direction + [zero])]
            product = following

    field = []
    for k in range(3):
        value = pressure[0] * basis[0][k]
        for j in range(1, ITERS):
            value = value + pressure[j] * basis[j][k]
        field.append(value)
    field_e = to_east(field)
    wet = [jnp.where(surface[k], 1.0, 0.0) for k in range(3)]
    wet_e = to_east(wet)
    for h in range(2):
        slope_e = wet[h] * wet_e[h] * (field_e[h] - field[h])
        slope_n = wet[h] * to_north(wet[h]) * (to_north(field[h]) - field[h])
        grad[0, :, 128 * h : 128 * h + 128] = slope_e[0:16]
        grad[1, :, 128 * h : 128 * h + 128] = slope_n[0:16]


def body(lats, lons, tracers, east_velocity, north_velocity, column_levels, surface_term):
    tall = 2 * LEVELS * ROWS
    cells = tracers.reshape(2 * LEVELS, ROWS, 256)
    east = east_velocity.reshape(LEVELS * ROWS, 256)
    north = north_velocity.reshape(LEVELS * ROWS, 256)
    size_a, size_b = lats // NZ, NZ * lons
    vmem = pltpu.VMEM
    scratch = [
        vmem((2, 2, LEVELS * ROWS, 128), BF16),
        vmem((2, 2, LEVELS * ROWS, 128), F32),
        vmem((ROWS, 256), jnp.int32),
        vmem((ROWS, 256), F32),
        vmem((HIGH, 2, 80, 128), F32),
        vmem((HIGH, 2, 80, 128), F32),
        vmem((HIGH, 2, 64, 128), F32),
        vmem((HIGH, 2, 64, 128), F32),
        vmem((2, 2, 64, 128), F32),
        vmem((HIGH, 2, 2, LEVELS, 128), F32),
        vmem((ROWS, 2, 64, 128), F32),
        vmem((HIGH, 8, 128), F32),
        vmem((HIGH, 8, 128), F32),
        vmem((HIGH, 8, 128), F32),
        vmem((HIGH, 8, 128), F32),
        vmem((ROWS, 8, 128), F32),
        vmem((ROWS, 8, 128), F32),
        vmem((2, 10, 8, 128), F32),
        vmem((2, 9, 8, 128), F32),
        vmem((4, 3, 8, 128), F32),
        vmem((2, 3, 2, 64, 128), BF16),
        vmem((2, 3, 2, 64, 128), BF16),
        vmem((3, 2, 2, LEVELS, 128), BF16),
        vmem((2, 2, 2, LEVELS, 128), BF16),
        vmem((3, 2, 2, LEVELS, 128), BF16),
        vmem((2, 2, 2, LEVELS, 128), BF16),
        vmem((2, 2, 2, 8, 128), F32),
        vmem((2, 2, 8, 128), F32),
        vmem((2, 2, 8, 128), F32),
        vmem((2, 2, 8, 128), F32),
        vmem((2, 8, 128), F32),
        vmem((2, 8, 128), F32),
        vmem((2, 8, 128), F32),
        vmem((2, 8, 128), F32),
        vmem((4, 8, 128), F32),
        vmem((2, 3, HIGH, 128), F32),
        vmem((ROWS, 2, 8, 128), F32),
        vmem((2, tall, 128), F32),
        vmem((1, 128), F32),
        vmem((size_a, 1, 128), F32),
        vmem((1, 128), F32),
        vmem((size_b, 1, 128), F32),
        pltpu.SemaphoreType.DMA((6 + 2 * ROWS,)),
        pltpu.SemaphoreType.DMA((15,)),
        pltpu.SemaphoreType.DMA((15,)),
        pltpu.SemaphoreType.DMA((8,)),
        pltpu.SemaphoreType.DMA((8,)),
        pltpu.SemaphoreType.DMA((size_a,)),
        pltpu.SemaphoreType.DMA((size_a,)),
        pltpu.SemaphoreType.DMA((size_b,)),
        pltpu.SemaphoreType.DMA((size_b,)),
    ]
    hbm, near = pl.BlockSpec(memory_space=pltpu.HBM), pl.BlockSpec(memory_space=pltpu.VMEM)
    updated, gradient = pl.pallas_call(
        functools.partial(kernel, lats, lons),
        out_shape=(pltpu.VMEM((tall, 256), F32), pltpu.VMEM((2, ROWS, 256), F32)),
        in_specs=[hbm] * 5,
        out_specs=(near, near),
        scratch_shapes=scratch,
        compiler_params=pltpu.CompilerParams(
            collective_id=0, has_side_effects=True, vmem_limit_bytes=40 * 1024 * 1024
        ),
    )(*[pltpu.with_memory_space_constraint(x, pltpu.HBM) for x in (cells, east, north, column_levels, surface_term)])
    return updated.reshape(2, LEVELS, ROWS, 256), gradient


def solution(mesh):
    in_specs = (
        P(None, None, "lat", "lon"),
        P(None, "lat", "lon"),
        P(None, "lat", "lon"),
        P("lat", "lon"),
        P("lat", "lon"),
    )
    out_specs = (P(None, None, "lat", "lon"), P(None, "lat", "lon"))
    step = functools.partial(body, mesh.shape["lat"], mesh.shape["lon"])
    return jax.shard_map(step, mesh=mesh, in_specs=in_specs, out_specs=out_specs, check_vma=False)
```

```python
import functools
import math

import jax
import jax.numpy as jnp
from jax import lax
from jax.experimental import pallas as pl
from jax.experimental.pallas import tpu as pltpu
from jax.sharding import PartitionSpec as P

MESH = pl.DeviceIdType.MESH
F32 = jnp.float32
BF16 = jnp.bfloat16

ITERS = 4
LEVELS = 32
ROWS = 16
HALO = 4
HIGH = ROWS + 2 * HALO
NX = 4
NZ = 2

time_step = 0.5
biharm_coef = 0.05
vertical_coef = 0.8


def iota(shape, axis):
    return lax.broadcasted_iota(jnp.int32, shape, axis)


def kernel(
    lats, lons, trc, vel_e, vel_n, levels_in, term_in, out, grad,
    vin, vf, levi, termi, X, M, LP, SX, GC, V, U, Xs, Ms, Us, Vs, Qt, Qv, pack, pack_in, corner_in,
    xb, xb_in, vbn, vbs, vbn_in, vbs_in, FL, FT, ft_in,
    FO, gn, gs, ge, gw, gc, MK, FS, tout, sa, ra, sb, rb,
    in_sem, s1, r1, s2, r2, sas, sar, sbs, sbr,
):
    la, lo = lax.axis_index("lat"), lax.axis_index("lon")
    north, south = lax.rem(la + 1, lats), lax.rem(la + lats - 1, lats)
    east, west = lax.rem(lo + 1, lons), lax.rem(lo + lons - 1, lons)
    ny = lats // (NX * NZ)
    y, zx = la // (NX * NZ), lax.rem(la, NX * NZ)
    zz, xx = zx // NX, lax.rem(zx, NX)
    size_a, size_b = ny * NX, NZ * lons
    me_a, me_b = y * NX + xx, zz * lons + lo

    def turns(value, count):
        return [value] + [jnp.where(value + d >= count, value + d - count, value + d) for d in range(1, count)]

    xs, ys, zs, ls = turns(xx, NX), turns(y, ny), turns(zz, NZ), turns(lo, lons)

    def partner_a(k):
        y_k, x_k = ys[k // NX], xs[k % NX]
        return ((y_k * NZ + zz) * NX + x_k, lo), y_k * NX + x_k

    def partner_b(k):
        z_k, l_k = zs[k // lons], ls[k % lons]
        return ((y * NZ + z_k) * NX + xx, l_k), z_k * lons + l_k

    barrier = pltpu.get_barrier_semaphore()
    around = [
        (north, east), (south, east), (north, west), (south, west),
        (north, lo), (south, lo), (la, east), (la, west),
    ]
    def ring(d, count):
        return min(d, count - d)

    far_a = sorted(range(1, size_a), key=lambda k: -ring(k // NX, ny) - ring(k % NX, NX))
    far_b = sorted(range(1, size_b), key=lambda k: -ring(k % lons, lons) - 0.5 * (k // lons))
    partners = [partner_a(k)[0] for k in far_a] + [partner_b(k)[0] for k in far_b]

    def greet(devices):
        for device in devices:
            pl.semaphore_signal(barrier, inc=1, device_id=device, device_id_type=MESH)

    greet(around)

    loads = [
        pltpu.make_async_copy(levels_in, levi, in_sem.at[0]),
        pltpu.make_async_copy(term_in, termi, in_sem.at[1]),
    ]
    edge_rows = [0, 1, 2, 3, 12, 13, 14, 15]
    inner_rows = list(range(4, 12))

    def load_rows(rows):
        return [
            pltpu.make_async_copy(
                trc.at[:, r, pl.ds(128 * h, 128)], X.at[r + HALO, h, pl.ds(8, 64)], in_sem.at[6 + 2 * r + h]
            )
            for r in rows
            for h in range(2)
        ]

    x_loads = load_rows(edge_rows)
    v_loads = [
        pltpu.make_async_copy(src.at[:, pl.ds(128 * h, 128)], vin.at[w, h], in_sem.at[2 + 2 * w + h])
        for w, src in enumerate((vel_e, vel_n))
        for h in range(2)
    ]
    y_loads = load_rows(inner_rows)
    for load in loads + x_loads + v_loads + y_loads:
        load.start()
    greet(partners)

    def send(src, dst, k, device, ss=s1, rr=r1):
        copy = pltpu.make_async_remote_copy(
            src_ref=src, dst_ref=dst, send_sem=ss.at[k], recv_sem=rr.at[k], device_id=device, device_id_type=MESH
        )
        copy.start()
        return copy

    lane = iota((8, 128), 1)
    sub = iota((8, 128), 0)
    lane16 = lax.rem(lane, 16)
    laneq = lane // 16

    def rows_of(first, last, step, carry=0, size=2):
        def group(n, carry):
            for r in range(size):
                carry = step(first + size * n + r, carry)
            return carry

        return lax.fori_loop(0, (last - first) // size, group, carry)

    for load in loads:
        load.wait()
    for h in range(2):
        for tile in range(2):
            FL[h, tile, 0] = levi[8 * tile : 8 * tile + 8, 128 * h : 128 * h + 128].astype(F32)
            FL[h, tile, 1] = termi[8 * tile : 8 * tile + 8, 128 * h : 128 * h + 128]

    for h in range(2):
        FT[0, h] = jnp.where(sub < 4, pltpu.roll(FL[h, 1, 0], 4, 0), FL[h, 1, 1])
        FT[1, h] = jnp.where(sub < 4, FL[h, 0, 0], pltpu.roll(FL[h, 0, 1], 4, 0))
    for side in range(2):
        packed = jnp.zeros((8, 128), F32)
        for f in range(2):
            for tile in range(2):
                j = 2 * f + tile
                turn = (4 * j + 4) % 128 if side == 0 else 4 * j
                value = FL[1 - side, tile, f]
                packed = jnp.where(lane // 4 == j, pltpu.roll(value, turn, 1) if turn else value, packed)
        pack[side, 0] = packed
        pack[side, 9] = packed

    for load in x_loads:
        load.wait()
    for j in range(3):
        xb[0, j] = X[16 + j, :, 8:72, :].astype(BF16)
        xb[1, j] = X[5 + j, :, 8:72, :].astype(BF16)

    for load in v_loads:
        load.wait()

    def widen(n, carry):
        rows = pl.ds(pl.multiple_of(64 * n, 64), 64)
        for w in range(2):
            for h in range(2):
                vf[w, h, rows, :] = vin[w, h, rows, :].astype(F32) * (0.5 * time_step)
        return carry

    lax.fori_loop(0, 8, widen, 0)

    def fill_v(i, carry):
        for w in range(2):
            for h in range(2):
                V[i, w, h] = vf[w, h, pl.ds(i - HALO, 32, stride=ROWS), :]
        return carry

    rows_of(HALO, HALO + ROWS, fill_v, size=4)
    for j in range(3):
        vbn[j] = V[17 + j].astype(BF16)
    for j in range(2):
        vbs[j] = V[4 + j].astype(BF16)

    def seam_of(parts):
        out = jnp.zeros((8, 128), F32)
        for q, (low, high) in enumerate(parts):
            both = jnp.where(lane >= 124, high, low)
            out = jnp.where(laneq == q, pltpu.roll(both, (16 * q + 4) % 128, 1), out)
        return out

    def seam_x(i):
        return seam_of([(X[i, 0, 8 * q + 8 : 8 * q + 16, :], X[i, 1, 8 * q + 8 : 8 * q + 16, :]) for q in range(8)])

    def seam_v(i):
        return seam_of(
            [
                (V[i, q // 4, 0, 8 * (q % 4) : 8 * (q % 4) + 8, :], V[i, q // 4, 1, 8 * (q % 4) : 8 * (q % 4) + 8, :])
                for q in range(8)
            ]
        )

    def pack_rows(i, carry):
        Qt[i - HALO] = seam_x(i)
        Qv[i - HALO] = seam_v(i)
        return carry

    for load in y_loads:
        load.wait()
    rows_of(HALO, HALO + ROWS, pack_rows, size=8)
    for a in range(4):
        for w, Q in enumerate((Qt, Qv)):
            for side in range(2):
                packed = jnp.zeros((8, 128), F32)
                for n in range(4):
                    turn = (4 * n - 4 * side) % 128
                    value = Q[4 * a + n]
                    packed = jnp.where(lane16 // 4 == n, pltpu.roll(value, turn, 1) if turn else value, packed)
                pack[side, 1 + 2 * a + w] = packed

    pl.semaphore_wait(barrier, len(around) + len(partners))

    body_rows = pl.ds(8, 64)
    c_side = [
        send(pack.at[0, pl.ds(0, 9)], pack_in.at[0], 0, (la, east)),
        send(pack.at[1, pl.ds(0, 9)], pack_in.at[1], 1, (la, west)),
    ]
    c_far = [
        send(pack.at[0, pl.ds(7, 3)], corner_in.at[0], 2, (north, east)),
        send(pack.at[0, pl.ds(0, 3)], corner_in.at[1], 3, (south, east)),
        send(pack.at[1, pl.ds(7, 3)], corner_in.at[2], 4, (north, west)),
        send(pack.at[1, pl.ds(0, 3)], corner_in.at[3], 5, (south, west)),
        send(FT.at[0], ft_in.at[0], 6, (north, lo)),
        send(FT.at[1], ft_in.at[1], 7, (south, lo)),
        send(X.at[19, :, body_rows], X.at[3, :, body_rows], 8, (north, lo)),
        send(X.at[4, :, body_rows], X.at[20, :, body_rows], 9, (south, lo)),
        send(xb.at[0], xb_in.at[0], 10, (north, lo)),
        send(xb.at[1], xb_in.at[1], 11, (south, lo)),
        send(vbn.at[pl.ds(1, 2)], vbn_in.at[pl.ds(1, 2)], 12, (north, lo)),
        send(vbn.at[0, 1], vbn_in.at[0, 1], 13, (north, lo)),
        send(vbs, vbs_in, 14, (south, lo)),
    ]

    def flat(own, n, s, e, w, ne, se, nw, sw):
        parts = [jnp.concatenate([own[h][0], own[h][1], jnp.where(sub < 4, n[h], s[h])], axis=0) for h in range(2)]
        right = jnp.concatenate([e[0], e[1], jnp.where(sub < 4, ne, se)], axis=0)
        left = jnp.concatenate([w[0], w[1], jnp.where(sub < 4, nw, sw)], axis=0)
        parts.append(jnp.where(iota((24, 128), 1) < 64, right, left))
        return parts

    def to_east(parts):
        rolled = [pltpu.roll(p, 127, 1) for p in parts]
        last = iota(parts[0].shape, 1) == 127
        return [jnp.where(last, rolled[(k + 1) % 3], rolled[k]) for k in range(3)]

    def to_west(parts):
        rolled = [pltpu.roll(p, 1, 1) for p in parts]
        first = iota(parts[0].shape, 1) == 0
        return [jnp.where(first, rolled[(k + 2) % 3], rolled[k]) for k in range(3)]

    def to_north(part):
        return pltpu.roll(part, 23, 0)

    def to_south(part):
        return pltpu.roll(part, 1, 0)

    def put_masks(depth):
        east_depth = to_east(depth)
        for h in range(2):
            MK[h, 0] = depth[h]
            MK[h, 1] = jnp.minimum(depth[h], east_depth[h])
            MK[h, 2] = jnp.minimum(depth[h], to_north(depth[h]))

    dry = jnp.zeros((8, 128), F32)
    put_masks([jnp.concatenate([FL[h, 0, 0], FL[h, 1, 0], dry], axis=0) for h in range(2)] + [jnp.zeros((24, 128), F32)])

    level = sub.astype(F32)
    mixing = time_step * biharm_coef
    lifting = time_step * vertical_coef

    def mask_row(h, n, i):
        return MK[h, n, pl.ds(jnp.where(i >= HALO, i - HALO, i + 20), 1), :]

    def at(ref, i, h, t, g, up=0):
        start = 8 + 32 * t + 8 * g + up
        return ref[i, h, start : start + 8, :]

    def bare(t, g):
        return slice(32 * t + 8 * g, 32 * t + 8 * g + 8)

    def shift_e(halves):
        low, high = pltpu.roll(halves[0], 127, 1), pltpu.roll(halves[1], 127, 1)
        return [jnp.where(lane == 127, high, low), high]

    def shift_w(halves):
        low, high = pltpu.roll(halves[0], 1, 1), pltpu.roll(halves[1], 1, 1)
        return [low, jnp.where(lane == 0, low, high)]

    def pull(rims, q):
        return None if rims is None else pltpu.roll(rims, (124 - 16 * q) % 128, 1)

    def laplace(ref, firsts, count, size=2):
        def group(ref, i):
            edge_e = [[mask_row(h, 1, i + r) for h in range(2)] for r in range(size)]
            edge_n = [[mask_row(h, 2, i + r) for h in range(2)] for r in range(-1, size)]
            for g in range(4):
                here = level + 8.0 * g
                wet_e = [[here < edge for edge in pair] for pair in edge_e]
                wet_n = [[here < edge for edge in pair] for pair in edge_n]
                for t in range(2):
                    x = [[at(ref, i + r, h, t, g) for h in range(2)] for r in range(-1, size + 1)]
                    north_flux = [
                        [jnp.where(wet_n[r][h], x[r + 1][h] - x[r][h], 0.0) for h in range(2)]
                        for r in range(size + 1)
                    ]
                    for r in range(size):
                        mid = x[r + 1]
                        xe = shift_e(mid)
                        flux = [jnp.where(wet_e[r][h], xe[h] - mid[h], 0.0) for h in range(2)]
                        flux_w = shift_w(flux)
                        for h in range(2):
                            SX[i + r, h, bare(t, g), :] = mid[h] + xe[h]
                            total = (flux[h] - flux_w[h]) + (north_flux[r + 1][h] - north_flux[r][h])
                            LP[i + r, h, bare(t, g), :] = mixing * total

        def step(n, carry):
            for first in firsts:
                group(ref, first + size * n)
            return carry

        lax.fori_loop(0, count // size, step, 0)

    def northward(ref, i, wet, x, xn, lap, lapn, h, g):
        value = V[i, 1, h, 8 * g : 8 * g + 8, :] * (x + xn) + (lapn - lap)
        return jnp.where(wet, value, 0.0)

    def tendency(ref, firsts, count, put, finish, begin=lambda i: None, size=2):
        for block, first in enumerate(firsts):
            edge = [mask_row(h, 2, first - 1) for h in range(2)]
            for g in range(4):
                for t in range(2):
                    for h in range(2):
                        GC[block, h, bare(t, g), :] = northward(
                            ref, first - 1, level + 8.0 * g < edge[h],
                            at(ref, first - 1, h, t, g), at(ref, first, h, t, g),
                            LP[first - 1, h, bare(t, g), :], LP[first, h, bare(t, g), :], h, g,
                        )

        def group(block, i):
            deep, edge_e, edge_n = [
                [[mask_row(h, k, i + r) for h in range(2)] for r in range(size)] for k in range(3)
            ]
            done = [[None, None] for _ in range(size)]
            rims = [begin(i + r) for r in range(size)]
            for g in range(4):
                here = level + 8.0 * g
                for t in range(2):
                    x = [[at(ref, i + r, h, t, g) for h in range(2)] for r in range(size + 1)]
                    lap = [[LP[i + r, h, bare(t, g), :] for h in range(2)] for r in range(size + 1)]
                    below = [GC[block, h, bare(t, g), :] for h in range(2)]
                    for r in range(size):
                        pulled = pull(rims[r], 4 * t + g)
                        lape = shift_e(lap[r])
                        flux = []
                        for h in range(2):
                            value = V[i + r, 0, h, 8 * g : 8 * g + 8, :] * SX[i + r, h, bare(t, g), :]
                            value += lape[h] - lap[r][h]
                            flux.append(jnp.where(here < edge_e[r][h], value, 0.0))
                        flux_w = shift_w(flux)
                        for h in range(2):
                            mid = x[r][h]
                            above = northward(
                                ref, i + r, here < edge_n[r][h], mid, x[r + 1][h], lap[r][h], lap[r + 1][h], h, g
                            )
                            total = (flux_w[h] - flux[h]) + (below[h] - above)
                            below[h] = above
                            up = jnp.where(here + 1.0 < deep[r][h], at(ref, i + r, h, t, g, 1) - mid, 0.0)
                            wet_d = here < deep[r][h]
                            if g == 0:
                                wet_d = jnp.logical_and(wet_d, sub > 0)
                            down = jnp.where(wet_d, mid - at(ref, i + r, h, t, g, -1), 0.0)
                            part = put(i + r, t, g, h, mid, total + lifting * (up - down), deep[r][h], pulled)
                            if part is not None:
                                done[r][h] = part if done[r][h] is None else done[r][h] + part
                    for h in range(2):
                        GC[block, h, bare(t, g), :] = below[h]
            for r in range(size):
                finish(i + r, done[r])

        def step(n, carry):
            for block, first in enumerate(firsts):
                group(block, first + size * n)
            return carry

        lax.fori_loop(0, count // size, step, 0)

    def put_middle(i, t, g, h, x, half, deep, pulled):
        M[i, h, 8 + 32 * t + 8 * g : 16 + 32 * t + 8 * g, :] = x + half

    def nothing(i, done):
        pass

    def rim(value):
        return jnp.where(lane16 < 4, value, pltpu.roll(value, 120, 1))

    def patched(value, pulled, h):
        return jnp.where(lane < 2, pulled, value) if h == 0 else jnp.where(lane >= 126, pulled, value)

    def patch_middle(i, carry):
        value = Ms[i]
        rims = rim(value)
        parts = []
        for q in range(8):
            pulled = pull(rims, q)
            pair = [patched(M[i, h, 8 * q + 8 : 8 * q + 16, :], pulled, h) for h in range(2)]
            for h in range(2):
                M[i, h, 8 * q + 8 : 8 * q + 16, :] = pair[h]
            parts.append(tuple(pair))
        own = seam_of(parts)
        own = jnp.where(lane16 < 4, own, pltpu.roll(own, 8, 1))
        Ms[i] = jnp.where(jnp.logical_and(lane16 >= 4, lane16 < 12), value, own)
        return carry

    def put_updated(i, t, g, h, m, half, deep, pulled):
        value = patched(0.5 * ((at(X, i, h, t, g) + m) + half), pulled, h)
        U[i - HALO, h, bare(t, g), :] = value
        part = jnp.where(level + 8.0 * g < deep, value, 0.0)
        return part if t == 0 else -0.5 * part

    def put_forcing(i, done):
        for h in range(2):
            FS[i - HALO, h] = done[h]

    def seam_row(own, from_east, from_west, n):
        value = jnp.where(lane16 < 4, own, pltpu.roll(own, 8, 1))
        right = pltpu.roll(from_east, (4 - 4 * n) % 128, 1) if n != 1 else from_east
        left = pltpu.roll(from_west, (8 - 4 * n) % 128, 1) if n != 2 else from_west
        value = jnp.where(lane16 // 4 == 1, right, value)
        return jnp.where(lane16 // 4 == 2, left, value)

    def put_velocity(i, both):
        other = pltpu.roll(both, 64, 1)
        Us[i] = jnp.where(lane < 64, both, other)
        Vs[i] = jnp.where(lane < 64, other, both)

    level_s = (sub + 8 * lax.rem(laneq, 4)).astype(F32)

    def seam_masks(depth, rows):
        wide = iota(depth[0].shape, 1)
        seam_e = jnp.where(wide >= 124, depth[1], depth[2])
        seam_w = jnp.where(wide >= 124, depth[2], depth[0])
        base = jnp.where(wide < 8, pltpu.roll(seam_e, 4, 1), pltpu.roll(seam_w, 12, 1))
        base = jnp.where(wide < 16, base, 0.0)
        for turn in (16, 32, 64):
            base = base + pltpu.roll(base, turn, 1)
        deep = jnp.stack([jnp.broadcast_to(base[r : r + 1, :], (8, 128)) for r in rows], axis=0)
        wet_e = level_s[None] < jnp.minimum(deep, pltpu.roll(deep, 127, 2))
        wet_n = level_s[None] < jnp.minimum(deep[:-1], deep[1:])
        return wet_e, wet_n, level_s[None] + 1.0 < deep

    def seam_tendency(ref, first, last, masks):
        wet_e, wet_n, wet_u = masks
        x = ref[first - 2 : last + 2]
        xe = pltpu.roll(x, 127, 2)
        flux = jnp.where(wet_e, xe - x, 0.0)
        flux_n = jnp.where(wet_n, x[1:] - x[:-1], 0.0)
        lap = mixing * ((flux - pltpu.roll(flux, 1, 2))[1:-1] + (flux_n[1:] - flux_n[:-1]))
        x, xe = x[1:-1], xe[1:-1]
        flux = Us[first:last] * (x + xe)[1:-1] + (pltpu.roll(lap, 127, 2) - lap)[1:-1]
        flux = jnp.where(wet_e[2:-2], flux, 0.0)
        flux_n = Vs[first - 1 : last] * (x[1:] + x[:-1]) + (lap[1:] - lap[:-1])
        flux_n = jnp.where(wet_n[1:-1], flux_n, 0.0)
        x = x[1:-1]
        turned = pltpu.roll(x, 112, 2)
        upper = jnp.where(sub[None] < 7, pltpu.roll(x, 7, 1), pltpu.roll(turned, 7, 1))
        up = jnp.where(wet_u[2:-2], upper - x, 0.0)
        turned = pltpu.roll(up, 16, 2)
        down = jnp.where(sub[None] > 0, pltpu.roll(up, 1, 1), pltpu.roll(turned, 1, 1))
        total = (pltpu.roll(flux, 1, 2) - flux) + (flux_n[:-1] - flux_n[1:])
        return x, total + lifting * (up - down)

    def part_of(masks, first, last):
        return masks[0][first:last], masks[1][first : last - 1], masks[2][first:last]

    def seam_middle(first, last, masks):
        x, half = seam_tendency(Xs, first, last, masks)
        Ms[first:last] = x + half

    def seam_updated(first, last, masks):
        m, half = seam_tendency(Ms, first, last, masks)
        Xs[first:last] = 0.5 * ((Xs[first:last] + m) + half)

    laplace(X, [5], 14)
    tendency(X, [6], 12, put_middle, nothing)

    for copy in c_side:
        copy.wait_recv()
    for a in range(4):
        for n in range(4):
            i = HALO + 4 * a + n
            Xs[i] = seam_row(Qt[4 * a + n], pack_in[1, 1 + 2 * a], pack_in[0, 1 + 2 * a], n)
            put_velocity(i, seam_row(Qv[4 * a + n], pack_in[1, 2 + 2 * a], pack_in[0, 2 + 2 * a], n))

    def beside(f, tile, right, left):
        j = 2 * f + tile
        right = pltpu.roll(right, 128 - 4 * j, 1) if j else right
        return jnp.where(lane < 64, right, pltpu.roll(left, 124 - 4 * j, 1))

    inside = [[jnp.concatenate([FL[h, tile, f] for tile in range(2)], axis=0) for h in range(2)] for f in range(2)]
    for f in range(2):
        inside[f].append(jnp.concatenate([beside(f, tile, pack_in[1, 0], pack_in[0, 0]) for tile in range(2)], axis=0))
    masks = seam_masks(inside[0], range(16))
    seam_middle(6, 18, masks)
    rows_of(6, 18, patch_middle, size=6)
    seam_updated(8, 16, part_of(masks, 2, 14))
    laplace(M, [7], 10)
    tendency(M, [8], 8, put_updated, put_forcing, lambda i: rim(Xs[i]))

    for copy in c_far[4:6]:
        copy.wait_recv()
    no_north = (sub < 4).astype(jnp.int32) * (la == lats - 1).astype(jnp.int32)
    no_south = (sub >= 4).astype(jnp.int32) * (la == 0).astype(jnp.int32)
    outside = (no_north + no_south) > 0
    rims = [[], []]
    for h in range(2):
        from_north, from_south = ft_in[1, h], ft_in[0, h]
        rims[0].append(jnp.where(outside, 0.0, jnp.where(sub < 4, from_north, pltpu.roll(from_south, 4, 0))))
        rims[1].append(jnp.where(sub < 4, pltpu.roll(from_north, 4, 0), from_south))
    depth = [jnp.concatenate([inside[0][h], rims[0][h]], axis=0) for h in range(2)]
    put_masks(depth + [jnp.zeros((24, 128), F32)])
    for copy in c_far[6:10]:
        copy.wait_recv()
    for j in range(3):
        X[j, :, 8:72, :] = xb_in[0, j].astype(F32)
        X[21 + j, :, 8:72, :] = xb_in[1, j].astype(F32)
    laplace(X, [1, 19], 4)
    rim_x = [(seam_x(n), seam_x(20 + n)) for n in range(4)]
    for copy in c_far[10:]:
        copy.wait_recv()
    for j in range(2):
        V[2 + j] = vbn_in[1 + j].astype(F32)
        V[20 + j] = vbs_in[j].astype(F32)
    V[1, 1] = vbn_in[0, 1].astype(F32)
    tendency(X, [2, 18], 4, put_middle, nothing)
    rim_v = [seam_v(n) for n in (1, 2, 3, 20, 21)]

    for copy in c_far[:4]:
        copy.wait_recv()
    for f in range(2):
        above = beside(f, 0, corner_in[3, 0], corner_in[1, 0])
        below = beside(f, 1, corner_in[2, 2], corner_in[0, 2])
        rims[f].append(jnp.where(sub < 4, above, below))
    rims[0][2] = jnp.where(outside, 0.0, rims[0][2])
    depth.append(jnp.concatenate([inside[0][2], rims[0][2]], axis=0))
    diagonal = [6.0 + jnp.concatenate([inside[1][k], rims[1][k]], axis=0) for k in range(3)]
    for n in range(4):
        Xs[n] = seam_row(rim_x[n][0], corner_in[2, 0], corner_in[0, 0], n)
        Xs[20 + n] = seam_row(rim_x[n][1], corner_in[3, 1], corner_in[1, 1], n)
    for n in range(1, 4):
        put_velocity(n, seam_row(rim_v[n - 1], corner_in[2, 1], corner_in[0, 1], n))
    for n in range(2):
        put_velocity(20 + n, seam_row(rim_v[3 + n], corner_in[3, 2], corner_in[1, 2], n))
    masks_low = seam_masks(depth, list(range(20, 24)) + list(range(6)))
    masks_high = seam_masks(depth, range(10, 20))
    seam_middle(2, 6, part_of(masks_low, 0, 8))
    seam_middle(18, 22, part_of(masks_high, 2, 10))
    for first in (2, 18):
        for r in range(4):
            patch_middle(first + r, 0)
    seam_updated(4, 8, part_of(masks_low, 2, 10))
    seam_updated(16, 20, part_of(masks_high, 0, 8))
    laplace(M, [3, 17], 4)
    tendency(M, [4, 16], 4, put_updated, put_forcing, lambda i: rim(Xs[i]))

    def forcing_rows(first, last, h):
        return jnp.sum(FS[first:last, h], axis=1) * (1.0 / math.sqrt(LEVELS))

    for h in range(2):
        for tile in range(2):
            FO[h, tile] = forcing_rows(8 * tile, 8 * tile + 8, h)
    c_forcing = [
        send(FO.at[1, 1], gc.at[0], 4, (north, east), s2, r2),
        send(FO.at[1, 0], gc.at[1], 5, (south, east), s2, r2),
        send(FO.at[0, 1], gc.at[2], 6, (north, west), s2, r2),
        send(FO.at[0, 0], gc.at[3], 7, (south, west), s2, r2),
        send(FO.at[:, 1], gs, 0, (north, lo), s2, r2),
        send(FO.at[:, 0], gn, 1, (south, lo), s2, r2),
    ]
    c_forcing += [
        send(FO.at[1], gw, 2, (la, east), s2, r2),
        send(FO.at[0], ge, 3, (la, west), s2, r2),
    ]


    def put_rows(i, carry):
        for h in range(2):
            tout[h, pl.ds(i, 64, stride=ROWS), :] = U[i, h]
        return carry

    def put_out(n, carry):
        rows = pl.ds(pl.multiple_of(128 * n, 128), 128)
        for h in range(2):
            out[rows, 128 * h : 128 * h + 128] = tout[h, rows, :]
        return carry

    rows_of(0, ROWS, put_rows)
    lax.fori_loop(0, 8, put_out, 0)
    row = iota((24, 128), 0)
    surface = [p > 0.0 for p in depth]
    inverse = [jnp.where(surface[k], 1.0 / diagonal[k], 0.0) for k in range(3)]
    weight = [jnp.where(row < 16, diagonal[k], 0.0) for k in range(2)]
    for copy in c_forcing:
        copy.wait_recv()
    forcing = flat(
        [[FO[h, tile] for tile in range(2)] for h in range(2)],
        [gn[h] for h in range(2)], [gs[h] for h in range(2)],
        [ge[tile] for tile in range(2)], [gw[tile] for tile in range(2)],
        gc[3], gc[2], gc[1], gc[0],
    )

    def apply_b(parts):
        columns = [to_north(p) + to_south(p) for p in parts]
        mixed = [p + 0.5 * c for p, c in zip(parts, columns)]
        e, w = to_east(mixed), to_west(mixed)
        return [inverse[k] * (columns[k] + e[k] + w[k]) for k in range(3)]

    basis = [[forcing[k] * inverse[k] for k in range(3)]]
    basis.append(apply_b(basis[0]))
    for j in range(2, ITERS + 1):
        image = apply_b(basis[j - 1])
        basis.append([2.0 * image[k] - basis[j - 2][k] for k in range(3)])

    def partial(left, right):
        total = left[0] * right[0] + left[1] * right[1]
        total = total[0:8] + total[8:16]
        return jnp.sum(total, axis=0, keepdims=True)

    rows = []
    for j in range(ITERS):
        weighted = [weight[k] * basis[j][k] for k in range(2)]
        rows.append(partial(weighted, basis[j]))
        rows.append(partial(weighted, basis[j + 1]))
    sums = jnp.sum(jnp.concatenate(rows, axis=0), axis=1, keepdims=True)
    sa[...] = jnp.sum(jnp.where(lane == sub, sums, 0.0), axis=0, keepdims=True)

    sent = c_side + c_far + c_forcing

    def gather(src, dst, me, size, order, partner, ss, rr):
        copies = []
        for k in order:
            device, place = partner(k)
            copy = pltpu.make_async_remote_copy(
                src_ref=src, dst_ref=dst.at[me], send_sem=ss.at[k], recv_sem=rr.at[me],
                device_id=device, device_id_type=MESH,
            )
            copy.start()
            arrival = pltpu.make_async_remote_copy(
                src_ref=src, dst_ref=dst.at[place], send_sem=ss.at[k], recv_sem=rr.at[place],
                device_id=device, device_id_type=MESH,
            )
            copies.append((copy, arrival))
        dst[me] = src[...]
        for copy, arrival in copies:
            arrival.wait_recv()
            sent.append(copy)
        parts = [dst[k] for k in range(size)]
        while len(parts) > 1:
            parts = [parts[k] + parts[k + 1] for k in range(0, len(parts) - 1, 2)] + parts[len(parts) - len(parts) % 2 :]
        return parts[0]

    sb[...] = gather(sa, ra, me_a, size_a, far_a, partner_a, sas, sar)
    total = gather(sb, rb, me_b, size_b, far_b, partner_b, sbs, sbr)
    inner = [jnp.broadcast_to(total[:, k : k + 1], (1, 128)) for k in range(8)]
    c = inner[:2] + [2.0 * inner[k] - inner[k % 2] for k in range(2, 8)]

    def gram(i, j):
        return 0.5 * (c[i + j] + c[abs(i - j)])

    def ratio(top, bottom):
        good = jnp.logical_and(bottom > 0.0, top > 0.0)
        return jnp.where(good, top / jnp.where(good, bottom, 1.0), 0.0)

    zero = jnp.zeros_like(c[0])
    resid = [jnp.ones_like(zero)]
    direction = list(resid)
    pressure = [zero] * ITERS
    product = c[0]
    for k in range(ITERS):
        image = list(direction) + [zero]
        for j, value in enumerate(direction):
            if j == 0:
                image[1] = image[1] - value
            else:
                image[j + 1] = image[j + 1] - 0.5 * value
                image[j - 1] = image[j - 1] - 0.5 * value
        bottom = zero
        for i, value in enumerate(direction):
            line = zero
            for j, other in enumerate(image):
                line = line + other * gram(i, j)
            bottom = bottom + value * line
        alpha = ratio(product, bottom)
        for j, value in enumerate(direction):
            pressure[j] = pressure[j] + alpha * value
        if k + 1 < ITERS:
            resid = [a - alpha * b for a, b in zip(resid + [zero], image)]
            following = zero
            for i, value in enumerate(resid):
                line = zero
                for j, other in enumerate(resid):
                    line = line + other * gram(i, j)
                following = following + value * line
            beta = ratio(following, product)
            direction = [a + beta * b for a, b in zip(resid, direction + [zero])]
            product = following

    field = []
    for k in range(3):
        value = pressure[0] * basis[0][k]
        for j in range(1, ITERS):
            value = value + pressure[j] * basis[j][k]
        field.append(value)
    field_e = to_east(field)
    wet = [jnp.where(surface[k], 1.0, 0.0) for k in range(3)]
    wet_e = to_east(wet)
    for h in range(2):
        slope_e = wet[h] * wet_e[h] * (field_e[h] - field[h])
        slope_n = wet[h] * to_north(wet[h]) * (to_north(field[h]) - field[h])
        grad[0, :, 128 * h : 128 * h + 128] = slope_e[0:16]
        grad[1, :, 128 * h : 128 * h + 128] = slope_n[0:16]
    for copy in sent:
        copy.wait_send()


def body(lats, lons, tracers, east_velocity, north_velocity, column_levels, surface_term):
    tall = 2 * LEVELS * ROWS
    cells = tracers.reshape(2 * LEVELS, ROWS, 256)
    east = east_velocity.reshape(LEVELS * ROWS, 256)
    north = north_velocity.reshape(LEVELS * ROWS, 256)
    size_a, size_b = lats // NZ, NZ * lons
    vmem = pltpu.VMEM
    scratch = [
        vmem((2, 2, LEVELS * ROWS, 128), BF16),
        vmem((2, 2, LEVELS * ROWS + ROWS, 128), F32),
        vmem((ROWS, 256), jnp.int32),
        vmem((ROWS, 256), F32),
        vmem((HIGH, 2, 80, 128), F32),
        vmem((HIGH, 2, 80, 128), F32),
        vmem((HIGH, 2, 64, 128), F32),
        vmem((HIGH, 2, 64, 128), F32),
        vmem((2, 2, 64, 128), F32),
        vmem((HIGH, 2, 2, LEVELS, 128), F32),
        vmem((ROWS, 2, 64, 128), F32),
        vmem((HIGH, 8, 128), F32),
        vmem((HIGH, 8, 128), F32),
        vmem((HIGH, 8, 128), F32),
        vmem((HIGH, 8, 128), F32),
        vmem((ROWS, 8, 128), F32),
        vmem((ROWS, 8, 128), F32),
        vmem((2, 10, 8, 128), F32),
        vmem((2, 9, 8, 128), F32),
        vmem((4, 3, 8, 128), F32),
        vmem((2, 3, 2, 64, 128), BF16),
        vmem((2, 3, 2, 64, 128), BF16),
        vmem((3, 2, 2, LEVELS, 128), BF16),
        vmem((2, 2, 2, LEVELS, 128), BF16),
        vmem((3, 2, 2, LEVELS, 128), BF16),
        vmem((2, 2, 2, LEVELS, 128), BF16),
        vmem((2, 2, 2, 8, 128), F32),
        vmem((2, 2, 8, 128), F32),
        vmem((2, 2, 8, 128), F32),
        vmem((2, 2, 8, 128), F32),
        vmem((2, 8, 128), F32),
        vmem((2, 8, 128), F32),
        vmem((2, 8, 128), F32),
        vmem((2, 8, 128), F32),
        vmem((4, 8, 128), F32),
        vmem((2, 3, HIGH, 128), F32),
        vmem((ROWS, 2, 8, 128), F32),
        vmem((2, tall + ROWS, 128), F32),
        vmem((1, 128), F32),
        vmem((size_a, 1, 128), F32),
        vmem((1, 128), F32),
        vmem((size_b, 1, 128), F32),
        pltpu.SemaphoreType.DMA((6 + 2 * ROWS,)),
        pltpu.SemaphoreType.DMA((15,)),
        pltpu.SemaphoreType.DMA((15,)),
        pltpu.SemaphoreType.DMA((8,)),
        pltpu.SemaphoreType.DMA((8,)),
        pltpu.SemaphoreType.DMA((size_a,)),
        pltpu.SemaphoreType.DMA((size_a,)),
        pltpu.SemaphoreType.DMA((size_b,)),
        pltpu.SemaphoreType.DMA((size_b,)),
    ]
    hbm, near = pl.BlockSpec(memory_space=pltpu.HBM), pl.BlockSpec(memory_space=pltpu.VMEM)
    updated, gradient = pl.pallas_call(
        functools.partial(kernel, lats, lons),
        out_shape=(pltpu.VMEM((tall, 256), F32), pltpu.VMEM((2, ROWS, 256), F32)),
        in_specs=[hbm] * 5,
        out_specs=(near, near),
        scratch_shapes=scratch,
        compiler_params=pltpu.CompilerParams(
            collective_id=0, has_side_effects=True, vmem_limit_bytes=40 * 1024 * 1024
        ),
    )(*[pltpu.with_memory_space_constraint(x, pltpu.HBM) for x in (cells, east, north, column_levels, surface_term)])
    return updated.reshape(2, LEVELS, ROWS, 256), gradient


def solution(mesh):
    in_specs = (
        P(None, None, "lat", "lon"),
        P(None, "lat", "lon"),
        P(None, "lat", "lon"),
        P("lat", "lon"),
        P("lat", "lon"),
    )
    out_specs = (P(None, None, "lat", "lon"), P(None, "lat", "lon"))
    step = functools.partial(body, mesh.shape["lat"], mesh.shape["lon"])
    return jax.shard_map(step, mesh=mesh, in_specs=in_specs, out_specs=out_specs, check_vma=False)
```

```python
import functools
import math

import jax
import jax.numpy as jnp
from jax import lax
from jax.experimental import pallas as pl
from jax.experimental.pallas import tpu as pltpu
from jax.sharding import PartitionSpec as P

MESH = pl.DeviceIdType.MESH
F32 = jnp.float32
BF16 = jnp.bfloat16

ITERS = 4
LEVELS = 32
ROWS = 16
HALO = 4
HIGH = ROWS + 2 * HALO
NX = 4
NZ = 2

time_step = 0.5
biharm_coef = 0.05
vertical_coef = 0.8


def iota(shape, axis):
    return lax.broadcasted_iota(jnp.int32, shape, axis)


def kernel(
    lats, lons, trc, vel_e, vel_n, levels_in, term_in, out, grad,
    vin, vf, levi, termi, X, M, LP, SX, GC, V, U, Xs, Ms, Us, Vs, Qt, Qv, pack, pack_in, corner_in,
    xb, xb_in, vbn, vbs, vbn_in, vbs_in, FL, FT, ft_in,
    FO, gn, gs, ge, gw, gc, MK, FS, tout, sa, ra, sb, rb,
    in_sem, s1, r1, s2, r2, sas, sar, sbs, sbr,
):
    la, lo = lax.axis_index("lat"), lax.axis_index("lon")
    north, south = lax.rem(la + 1, lats), lax.rem(la + lats - 1, lats)
    east, west = lax.rem(lo + 1, lons), lax.rem(lo + lons - 1, lons)
    ny = lats // (NX * NZ)
    y, zx = la // (NX * NZ), lax.rem(la, NX * NZ)
    zz, xx = zx // NX, lax.rem(zx, NX)
    size_a, size_b = ny * NX, NZ * lons
    me_a, me_b = y * NX + xx, zz * lons + lo

    def turns(value, count):
        return [value] + [jnp.where(value + d >= count, value + d - count, value + d) for d in range(1, count)]

    xs, ys, zs, ls = turns(xx, NX), turns(y, ny), turns(zz, NZ), turns(lo, lons)

    def partner_a(k):
        y_k, x_k = ys[k // NX], xs[k % NX]
        return ((y_k * NZ + zz) * NX + x_k, lo), y_k * NX + x_k

    def partner_b(k):
        z_k, l_k = zs[k // lons], ls[k % lons]
        return ((y * NZ + z_k) * NX + xx, l_k), z_k * lons + l_k

    barrier = pltpu.get_barrier_semaphore()
    around = [
        (north, east), (south, east), (north, west), (south, west),
        (north, lo), (south, lo), (la, east), (la, west),
    ]
    def ring(d, count):
        return min(d, count - d)

    far_a = sorted(range(1, size_a), key=lambda k: -ring(k // NX, ny) - ring(k % NX, NX))
    far_b = sorted(range(1, size_b), key=lambda k: -ring(k % lons, lons) - 0.5 * (k // lons))
    partners = [partner_a(k)[0] for k in far_a] + [partner_b(k)[0] for k in far_b]

    def greet(devices):
        for device in devices:
            pl.semaphore_signal(barrier, inc=1, device_id=device, device_id_type=MESH)

    greet(around)
    greet(partners)

    loads = [
        pltpu.make_async_copy(levels_in, levi, in_sem.at[0]),
        pltpu.make_async_copy(term_in, termi, in_sem.at[1]),
    ]
    edge_rows = [0, 1, 2, 3, 12, 13, 14, 15]
    inner_rows = list(range(4, 12))

    def load_rows(rows):
        return [
            pltpu.make_async_copy(
                trc.at[:, r, pl.ds(128 * h, 128)], X.at[r + HALO, h, pl.ds(8, 64)], in_sem.at[6 + 2 * r + h]
            )
            for r in rows
            for h in range(2)
        ]

    x_loads = load_rows(edge_rows)
    v_loads = [
        pltpu.make_async_copy(src.at[:, pl.ds(128 * h, 128)], vin.at[w, h], in_sem.at[2 + 2 * w + h])
        for w, src in enumerate((vel_e, vel_n))
        for h in range(2)
    ]
    y_loads = load_rows(inner_rows)
    for load in loads + x_loads + v_loads + y_loads:
        load.start()
    def send(src, dst, k, device, ss=s1, rr=r1):
        copy = pltpu.make_async_remote_copy(
            src_ref=src, dst_ref=dst, send_sem=ss.at[k], recv_sem=rr.at[k], device_id=device, device_id_type=MESH
        )
        copy.start()
        return copy

    lane = iota((8, 128), 1)
    sub = iota((8, 128), 0)
    lane16 = lax.rem(lane, 16)
    laneq = lane // 16

    def rows_of(first, last, step, carry=0, size=2):
        def group(n, carry):
            for r in range(size):
                carry = step(first + size * n + r, carry)
            return carry

        return lax.fori_loop(0, (last - first) // size, group, carry)

    for load in loads:
        load.wait()
    for h in range(2):
        for tile in range(2):
            FL[h, tile, 0] = levi[8 * tile : 8 * tile + 8, 128 * h : 128 * h + 128].astype(F32)
            FL[h, tile, 1] = termi[8 * tile : 8 * tile + 8, 128 * h : 128 * h + 128]

    for h in range(2):
        FT[0, h] = jnp.where(sub < 4, pltpu.roll(FL[h, 1, 0], 4, 0), FL[h, 1, 1])
        FT[1, h] = jnp.where(sub < 4, FL[h, 0, 0], pltpu.roll(FL[h, 0, 1], 4, 0))
    for side in range(2):
        packed = jnp.zeros((8, 128), F32)
        for f in range(2):
            for tile in range(2):
                j = 2 * f + tile
                turn = (4 * j + 4) % 128 if side == 0 else 4 * j
                value = FL[1 - side, tile, f]
                packed = jnp.where(lane // 4 == j, pltpu.roll(value, turn, 1) if turn else value, packed)
        pack[side, 0] = packed
        pack[side, 9] = packed

    for load in x_loads:
        load.wait()
    for j in range(3):
        xb[0, j] = X[16 + j, :, 8:72, :].astype(BF16)
        xb[1, j] = X[5 + j, :, 8:72, :].astype(BF16)

    for load in v_loads:
        load.wait()

    def widen(n, carry):
        rows = pl.ds(pl.multiple_of(64 * n, 64), 64)
        for w in range(2):
            for h in range(2):
                vf[w, h, rows, :] = vin[w, h, rows, :].astype(F32) * (0.5 * time_step)
        return carry

    lax.fori_loop(0, 8, widen, 0)

    def fill_v(i, carry):
        for w in range(2):
            for h in range(2):
                V[i, w, h] = vf[w, h, pl.ds(i - HALO, 32, stride=ROWS), :]
        return carry

    rows_of(HALO, HALO + ROWS, fill_v, size=4)
    for j in range(3):
        vbn[j] = V[17 + j].astype(BF16)
    for j in range(2):
        vbs[j] = V[4 + j].astype(BF16)

    def seam_of(parts):
        out = jnp.zeros((8, 128), F32)
        for q, (low, high) in enumerate(parts):
            both = jnp.where(lane >= 124, high, low)
            out = jnp.where(laneq == q, pltpu.roll(both, (16 * q + 4) % 128, 1), out)
        return out

    def seam_x(i):
        return seam_of([(X[i, 0, 8 * q + 8 : 8 * q + 16, :], X[i, 1, 8 * q + 8 : 8 * q + 16, :]) for q in range(8)])

    def seam_v(i):
        return seam_of(
            [
                (V[i, q // 4, 0, 8 * (q % 4) : 8 * (q % 4) + 8, :], V[i, q // 4, 1, 8 * (q % 4) : 8 * (q % 4) + 8, :])
                for q in range(8)
            ]
        )

    def pack_rows(i, carry):
        Qt[i - HALO] = seam_x(i)
        Qv[i - HALO] = seam_v(i)
        return carry

    for load in y_loads:
        load.wait()
    rows_of(HALO, HALO + ROWS, pack_rows, size=8)
    for a in range(4):
        for w, Q in enumerate((Qt, Qv)):
            for side in range(2):
                packed = jnp.zeros((8, 128), F32)
                for n in range(4):
                    turn = (4 * n - 4 * side) % 128
                    value = Q[4 * a + n]
                    packed = jnp.where(lane16 // 4 == n, pltpu.roll(value, turn, 1) if turn else value, packed)
                pack[side, 1 + 2 * a + w] = packed

    pl.semaphore_wait(barrier, len(around) + len(partners))

    body_rows = pl.ds(8, 64)
    c_side = [
        send(pack.at[0, pl.ds(0, 9)], pack_in.at[0], 0, (la, east)),
        send(pack.at[1, pl.ds(0, 9)], pack_in.at[1], 1, (la, west)),
    ]
    c_far = [
        send(pack.at[0, pl.ds(7, 3)], corner_in.at[0], 2, (north, east)),
        send(pack.at[0, pl.ds(0, 3)], corner_in.at[1], 3, (south, east)),
        send(pack.at[1, pl.ds(7, 3)], corner_in.at[2], 4, (north, west)),
        send(pack.at[1, pl.ds(0, 3)], corner_in.at[3], 5, (south, west)),
        send(FT.at[0], ft_in.at[0], 6, (north, lo)),
        send(FT.at[1], ft_in.at[1], 7, (south, lo)),
        send(X.at[19, :, body_rows], X.at[3, :, body_rows], 8, (north, lo)),
        send(X.at[4, :, body_rows], X.at[20, :, body_rows], 9, (south, lo)),
        send(xb.at[0], xb_in.at[0], 10, (north, lo)),
        send(xb.at[1], xb_in.at[1], 11, (south, lo)),
        send(vbn.at[pl.ds(1, 2)], vbn_in.at[pl.ds(1, 2)], 12, (north, lo)),
        send(vbn.at[0, 1], vbn_in.at[0, 1], 13, (north, lo)),
        send(vbs, vbs_in, 14, (south, lo)),
    ]

    def flat(own, n, s, e, w, ne, se, nw, sw):
        parts = [jnp.concatenate([own[h][0], own[h][1], jnp.where(sub < 4, n[h], s[h])], axis=0) for h in range(2)]
        right = jnp.concatenate([e[0], e[1], jnp.where(sub < 4, ne, se)], axis=0)
        left = jnp.concatenate([w[0], w[1], jnp.where(sub < 4, nw, sw)], axis=0)
        parts.append(jnp.where(iota((24, 128), 1) < 64, right, left))
        return parts

    def to_east(parts):
        rolled = [pltpu.roll(p, 127, 1) for p in parts]
        last = iota(parts[0].shape, 1) == 127
        return [jnp.where(last, rolled[(k + 1) % 3], rolled[k]) for k in range(3)]

    def to_west(parts):
        rolled = [pltpu.roll(p, 1, 1) for p in parts]
        first = iota(parts[0].shape, 1) == 0
        return [jnp.where(first, rolled[(k + 2) % 3], rolled[k]) for k in range(3)]

    def to_north(part):
        return pltpu.roll(part, 23, 0)

    def to_south(part):
        return pltpu.roll(part, 1, 0)

    def put_masks(depth):
        east_depth = to_east(depth)
        for h in range(2):
            MK[h, 0] = depth[h]
            MK[h, 1] = jnp.minimum(depth[h], east_depth[h])
            MK[h, 2] = jnp.minimum(depth[h], to_north(depth[h]))

    dry = jnp.zeros((8, 128), F32)
    put_masks([jnp.concatenate([FL[h, 0, 0], FL[h, 1, 0], dry], axis=0) for h in range(2)] + [jnp.zeros((24, 128), F32)])

    level = sub.astype(F32)
    mixing = time_step * biharm_coef
    lifting = time_step * vertical_coef

    def mask_row(h, n, i):
        return MK[h, n, pl.ds(jnp.where(i >= HALO, i - HALO, i + 20), 1), :]

    def at(ref, i, h, t, g, up=0):
        start = 8 + 32 * t + 8 * g + up
        return ref[i, h, start : start + 8, :]

    def bare(t, g):
        return slice(32 * t + 8 * g, 32 * t + 8 * g + 8)

    def shift_e(halves):
        low, high = pltpu.roll(halves[0], 127, 1), pltpu.roll(halves[1], 127, 1)
        return [jnp.where(lane == 127, high, low), high]

    def shift_w(halves):
        low, high = pltpu.roll(halves[0], 1, 1), pltpu.roll(halves[1], 1, 1)
        return [low, jnp.where(lane == 0, low, high)]

    def pull(rims, q):
        return None if rims is None else pltpu.roll(rims, (124 - 16 * q) % 128, 1)

    def laplace(ref, firsts, count, size=2):
        def group(ref, i):
            edge_e = [[mask_row(h, 1, i + r) for h in range(2)] for r in range(size)]
            edge_n = [[mask_row(h, 2, i + r) for h in range(2)] for r in range(-1, size)]
            for g in range(4):
                here = level + 8.0 * g
                wet_e = [[here < edge for edge in pair] for pair in edge_e]
                wet_n = [[here < edge for edge in pair] for pair in edge_n]
                for t in range(2):
                    x = [[at(ref, i + r, h, t, g) for h in range(2)] for r in range(-1, size + 1)]
                    north_flux = [
                        [jnp.where(wet_n[r][h], x[r + 1][h] - x[r][h], 0.0) for h in range(2)]
                        for r in range(size + 1)
                    ]
                    for r in range(size):
                        mid = x[r + 1]
                        xe = shift_e(mid)
                        flux = [jnp.where(wet_e[r][h], xe[h] - mid[h], 0.0) for h in range(2)]
                        flux_w = shift_w(flux)
                        for h in range(2):
                            SX[i + r, h, bare(t, g), :] = mid[h] + xe[h]
                            total = (flux[h] - flux_w[h]) + (north_flux[r + 1][h] - north_flux[r][h])
                            LP[i + r, h, bare(t, g), :] = mixing * total

        def step(n, carry):
            for first in firsts:
                group(ref, first + size * n)
            return carry

        lax.fori_loop(0, count // size, step, 0)

    def northward(ref, i, wet, x, xn, lap, lapn, h, g):
        value = V[i, 1, h, 8 * g : 8 * g + 8, :] * (x + xn) + (lapn - lap)
        return jnp.where(wet, value, 0.0)

    def tendency(ref, firsts, count, put, finish, begin=lambda i: None, size=2):
        for block, first in enumerate(firsts):
            edge = [mask_row(h, 2, first - 1) for h in range(2)]
            for g in range(4):
                for t in range(2):
                    for h in range(2):
                        GC[block, h, bare(t, g), :] = northward(
                            ref, first - 1, level + 8.0 * g < edge[h],
                            at(ref, first - 1, h, t, g), at(ref, first, h, t, g),
                            LP[first - 1, h, bare(t, g), :], LP[first, h, bare(t, g), :], h, g,
                        )

        def group(block, i):
            deep, edge_e, edge_n = [
                [[mask_row(h, k, i + r) for h in range(2)] for r in range(size)] for k in range(3)
            ]
            done = [[None, None] for _ in range(size)]
            rims = [begin(i + r) for r in range(size)]
            for g in range(4):
                here = level + 8.0 * g
                for t in range(2):
                    x = [[at(ref, i + r, h, t, g) for h in range(2)] for r in range(size + 1)]
                    lap = [[LP[i + r, h, bare(t, g), :] for h in range(2)] for r in range(size + 1)]
                    below = [GC[block, h, bare(t, g), :] for h in range(2)]
                    for r in range(size):
                        pulled = pull(rims[r], 4 * t + g)
                        lape = shift_e(lap[r])
                        flux = []
                        for h in range(2):
                            value = V[i + r, 0, h, 8 * g : 8 * g + 8, :] * SX[i + r, h, bare(t, g), :]
                            value += lape[h] - lap[r][h]
                            flux.append(jnp.where(here < edge_e[r][h], value, 0.0))
                        flux_w = shift_w(flux)
                        for h in range(2):
                            mid = x[r][h]
                            above = northward(
                                ref, i + r, here < edge_n[r][h], mid, x[r + 1][h], lap[r][h], lap[r + 1][h], h, g
                            )
                            total = (flux_w[h] - flux[h]) + (below[h] - above)
                            below[h] = above
                            up = jnp.where(here + 1.0 < deep[r][h], at(ref, i + r, h, t, g, 1) - mid, 0.0)
                            wet_d = here < deep[r][h]
                            if g == 0:
                                wet_d = jnp.logical_and(wet_d, sub > 0)
                            down = jnp.where(wet_d, mid - at(ref, i + r, h, t, g, -1), 0.0)
                            part = put(i + r, t, g, h, mid, total + lifting * (up - down), deep[r][h], pulled)
                            if part is not None:
                                done[r][h] = part if done[r][h] is None else done[r][h] + part
                    for h in range(2):
                        GC[block, h, bare(t, g), :] = below[h]
            for r in range(size):
                finish(i + r, done[r])

        def step(n, carry):
            for block, first in enumerate(firsts):
                group(block, first + size * n)
            return carry

        lax.fori_loop(0, count // size, step, 0)

    def put_middle(i, t, g, h, x, half, deep, pulled):
        M[i, h, 8 + 32 * t + 8 * g : 16 + 32 * t + 8 * g, :] = x + half

    def nothing(i, done):
        pass

    def rim(value):
        return jnp.where(lane16 < 4, value, pltpu.roll(value, 120, 1))

    def patched(value, pulled, h):
        return jnp.where(lane < 2, pulled, value) if h == 0 else jnp.where(lane >= 126, pulled, value)

    def patch_middle(i, carry):
        value = Ms[i]
        rims = rim(value)
        parts = []
        for q in range(8):
            pulled = pull(rims, q)
            pair = [patched(M[i, h, 8 * q + 8 : 8 * q + 16, :], pulled, h) for h in range(2)]
            for h in range(2):
                M[i, h, 8 * q + 8 : 8 * q + 16, :] = pair[h]
            parts.append(tuple(pair))
        own = seam_of(parts)
        own = jnp.where(lane16 < 4, own, pltpu.roll(own, 8, 1))
        Ms[i] = jnp.where(jnp.logical_and(lane16 >= 4, lane16 < 12), value, own)
        return carry

    def put_updated(i, t, g, h, m, half, deep, pulled):
        value = patched(0.5 * ((at(X, i, h, t, g) + m) + half), pulled, h)
        U[i - HALO, h, bare(t, g), :] = value
        part = jnp.where(level + 8.0 * g < deep, value, 0.0)
        return part if t == 0 else -0.5 * part

    def put_forcing(i, done):
        for h in range(2):
            FS[i - HALO, h] = done[h]

    def seam_row(own, from_east, from_west, n):
        value = jnp.where(lane16 < 4, own, pltpu.roll(own, 8, 1))
        right = pltpu.roll(from_east, (4 - 4 * n) % 128, 1) if n != 1 else from_east
        left = pltpu.roll(from_west, (8 - 4 * n) % 128, 1) if n != 2 else from_west
        value = jnp.where(lane16 // 4 == 1, right, value)
        return jnp.where(lane16 // 4 == 2, left, value)

    def put_velocity(i, both):
        other = pltpu.roll(both, 64, 1)
        Us[i] = jnp.where(lane < 64, both, other)
        Vs[i] = jnp.where(lane < 64, other, both)

    level_s = (sub + 8 * lax.rem(laneq, 4)).astype(F32)

    def seam_masks(depth, rows):
        wide = iota(depth[0].shape, 1)
        seam_e = jnp.where(wide >= 124, depth[1], depth[2])
        seam_w = jnp.where(wide >= 124, depth[2], depth[0])
        base = jnp.where(wide < 8, pltpu.roll(seam_e, 4, 1), pltpu.roll(seam_w, 12, 1))
        base = jnp.where(wide < 16, base, 0.0)
        for turn in (16, 32, 64):
            base = base + pltpu.roll(base, turn, 1)
        deep = jnp.stack([jnp.broadcast_to(base[r : r + 1, :], (8, 128)) for r in rows], axis=0)
        wet_e = level_s[None] < jnp.minimum(deep, pltpu.roll(deep, 127, 2))
        wet_n = level_s[None] < jnp.minimum(deep[:-1], deep[1:])
        return wet_e, wet_n, level_s[None] + 1.0 < deep

    def seam_tendency(ref, first, last, masks):
        wet_e, wet_n, wet_u = masks
        x = ref[first - 2 : last + 2]
        xe = pltpu.roll(x, 127, 2)
        flux = jnp.where(wet_e, xe - x, 0.0)
        flux_n = jnp.where(wet_n, x[1:] - x[:-1], 0.0)
        lap = mixing * ((flux - pltpu.roll(flux, 1, 2))[1:-1] + (flux_n[1:] - flux_n[:-1]))
        x, xe = x[1:-1], xe[1:-1]
        flux = Us[first:last] * (x + xe)[1:-1] + (pltpu.roll(lap, 127, 2) - lap)[1:-1]
        flux = jnp.where(wet_e[2:-2], flux, 0.0)
        flux_n = Vs[first - 1 : last] * (x[1:] + x[:-1]) + (lap[1:] - lap[:-1])
        flux_n = jnp.where(wet_n[1:-1], flux_n, 0.0)
        x = x[1:-1]
        turned = pltpu.roll(x, 112, 2)
        upper = jnp.where(sub[None] < 7, pltpu.roll(x, 7, 1), pltpu.roll(turned, 7, 1))
        up = jnp.where(wet_u[2:-2], upper - x, 0.0)
        turned = pltpu.roll(up, 16, 2)
        down = jnp.where(sub[None] > 0, pltpu.roll(up, 1, 1), pltpu.roll(turned, 1, 1))
        total = (pltpu.roll(flux, 1, 2) - flux) + (flux_n[:-1] - flux_n[1:])
        return x, total + lifting * (up - down)

    def part_of(masks, first, last):
        return masks[0][first:last], masks[1][first : last - 1], masks[2][first:last]

    def seam_middle(first, last, masks):
        x, half = seam_tendency(Xs, first, last, masks)
        Ms[first:last] = x + half

    def seam_updated(first, last, masks):
        m, half = seam_tendency(Ms, first, last, masks)
        Xs[first:last] = 0.5 * ((Xs[first:last] + m) + half)

    laplace(X, [5], 14)
    tendency(X, [6], 12, put_middle, nothing)

    for copy in c_side:
        copy.wait()
    for a in range(4):
        for n in range(4):
            i = HALO + 4 * a + n
            Xs[i] = seam_row(Qt[4 * a + n], pack_in[1, 1 + 2 * a], pack_in[0, 1 + 2 * a], n)
            put_velocity(i, seam_row(Qv[4 * a + n], pack_in[1, 2 + 2 * a], pack_in[0, 2 + 2 * a], n))

    def beside(f, tile, right, left):
        j = 2 * f + tile
        right = pltpu.roll(right, 128 - 4 * j, 1) if j else right
        return jnp.where(lane < 64, right, pltpu.roll(left, 124 - 4 * j, 1))

    inside = [[jnp.concatenate([FL[h, tile, f] for tile in range(2)], axis=0) for h in range(2)] for f in range(2)]
    for f in range(2):
        inside[f].append(jnp.concatenate([beside(f, tile, pack_in[1, 0], pack_in[0, 0]) for tile in range(2)], axis=0))
    masks = seam_masks(inside[0], range(16))
    seam_middle(6, 18, masks)
    rows_of(6, 18, patch_middle, size=6)
    seam_updated(8, 16, part_of(masks, 2, 14))
    laplace(M, [7], 10)
    tendency(M, [8], 8, put_updated, put_forcing, lambda i: rim(Xs[i]))

    for copy in c_far[4:6]:
        copy.wait()
    no_north = (sub < 4).astype(jnp.int32) * (la == lats - 1).astype(jnp.int32)
    no_south = (sub >= 4).astype(jnp.int32) * (la == 0).astype(jnp.int32)
    outside = (no_north + no_south) > 0
    rims = [[], []]
    for h in range(2):
        from_north, from_south = ft_in[1, h], ft_in[0, h]
        rims[0].append(jnp.where(outside, 0.0, jnp.where(sub < 4, from_north, pltpu.roll(from_south, 4, 0))))
        rims[1].append(jnp.where(sub < 4, pltpu.roll(from_north, 4, 0), from_south))
    depth = [jnp.concatenate([inside[0][h], rims[0][h]], axis=0) for h in range(2)]
    put_masks(depth + [jnp.zeros((24, 128), F32)])
    for copy in c_far[6:10]:
        copy.wait()
    for j in range(3):
        X[j, :, 8:72, :] = xb_in[0, j].astype(F32)
        X[21 + j, :, 8:72, :] = xb_in[1, j].astype(F32)
    laplace(X, [1, 19], 4)
    for copy in c_far[10:]:
        copy.wait()
    for j in range(2):
        V[2 + j] = vbn_in[1 + j].astype(F32)
        V[20 + j] = vbs_in[j].astype(F32)
    V[1, 1] = vbn_in[0, 1].astype(F32)
    tendency(X, [2, 18], 4, put_middle, nothing)

    for copy in c_far[:4]:
        copy.wait()
    for f in range(2):
        above = beside(f, 0, corner_in[3, 0], corner_in[1, 0])
        below = beside(f, 1, corner_in[2, 2], corner_in[0, 2])
        rims[f].append(jnp.where(sub < 4, above, below))
    rims[0][2] = jnp.where(outside, 0.0, rims[0][2])
    depth.append(jnp.concatenate([inside[0][2], rims[0][2]], axis=0))
    diagonal = [6.0 + jnp.concatenate([inside[1][k], rims[1][k]], axis=0) for k in range(3)]
    for n in range(4):
        Xs[n] = seam_row(seam_x(n), corner_in[2, 0], corner_in[0, 0], n)
        Xs[20 + n] = seam_row(seam_x(20 + n), corner_in[3, 1], corner_in[1, 1], n)
    for n in range(1, 4):
        put_velocity(n, seam_row(seam_v(n), corner_in[2, 1], corner_in[0, 1], n))
    for n in range(2):
        put_velocity(20 + n, seam_row(seam_v(20 + n), corner_in[3, 2], corner_in[1, 2], n))
    masks_low = seam_masks(depth, list(range(20, 24)) + list(range(6)))
    masks_high = seam_masks(depth, range(10, 20))
    seam_middle(2, 6, part_of(masks_low, 0, 8))
    seam_middle(18, 22, part_of(masks_high, 2, 10))
    for first in (2, 18):
        for r in range(4):
            patch_middle(first + r, 0)
    seam_updated(4, 8, part_of(masks_low, 2, 10))
    seam_updated(16, 20, part_of(masks_high, 0, 8))
    laplace(M, [3, 17], 4)
    tendency(M, [4, 16], 4, put_updated, put_forcing, lambda i: rim(Xs[i]))

    def forcing_rows(first, last, h):
        return jnp.sum(FS[first:last, h], axis=1) * (1.0 / math.sqrt(LEVELS))

    for h in range(2):
        for tile in range(2):
            FO[h, tile] = forcing_rows(8 * tile, 8 * tile + 8, h)
    c_forcing = [
        send(FO.at[1, 1], gc.at[0], 4, (north, east), s2, r2),
        send(FO.at[1, 0], gc.at[1], 5, (south, east), s2, r2),
        send(FO.at[0, 1], gc.at[2], 6, (north, west), s2, r2),
        send(FO.at[0, 0], gc.at[3], 7, (south, west), s2, r2),
        send(FO.at[:, 1], gs, 0, (north, lo), s2, r2),
        send(FO.at[:, 0], gn, 1, (south, lo), s2, r2),
    ]
    c_forcing += [
        send(FO.at[1], gw, 2, (la, east), s2, r2),
        send(FO.at[0], ge, 3, (la, west), s2, r2),
    ]


    def put_rows(i, carry):
        for h in range(2):
            tout[h, pl.ds(i, 64, stride=ROWS), :] = U[i, h]
        return carry

    def put_out(n, carry):
        rows = pl.ds(pl.multiple_of(128 * n, 128), 128)
        for h in range(2):
            out[rows, 128 * h : 128 * h + 128] = tout[h, rows, :]
        return carry

    rows_of(0, ROWS, put_rows)
    lax.fori_loop(0, 8, put_out, 0)
    row = iota((24, 128), 0)
    surface = [p > 0.0 for p in depth]
    inverse = [jnp.where(surface[k], 1.0 / diagonal[k], 0.0) for k in range(3)]
    weight = [jnp.where(row < 16, diagonal[k], 0.0) for k in range(2)]
    for copy in c_forcing:
        copy.wait()
    forcing = flat(
        [[FO[h, tile] for tile in range(2)] for h in range(2)],
        [gn[h] for h in range(2)], [gs[h] for h in range(2)],
        [ge[tile] for tile in range(2)], [gw[tile] for tile in range(2)],
        gc[3], gc[2], gc[1], gc[0],
    )

    def apply_b(parts):
        columns = [to_north(p) + to_south(p) for p in parts]
        mixed = [p + 0.5 * c for p, c in zip(parts, columns)]
        e, w = to_east(mixed), to_west(mixed)
        return [inverse[k] * (columns[k] + e[k] + w[k]) for k in range(3)]

    basis = [[forcing[k] * inverse[k] for k in range(3)]]
    basis.append(apply_b(basis[0]))
    for j in range(2, ITERS + 1):
        image = apply_b(basis[j - 1])
        basis.append([2.0 * image[k] - basis[j - 2][k] for k in range(3)])

    def partial(left, right):
        total = left[0] * right[0] + left[1] * right[1]
        total = total[0:8] + total[8:16]
        return jnp.sum(total, axis=0, keepdims=True)

    rows = []
    for j in range(ITERS):
        weighted = [weight[k] * basis[j][k] for k in range(2)]
        rows.append(partial(weighted, basis[j]))
        rows.append(partial(weighted, basis[j + 1]))
    sums = jnp.sum(jnp.concatenate(rows, axis=0), axis=1, keepdims=True)
    sa[...] = jnp.sum(jnp.where(lane == sub, sums, 0.0), axis=0, keepdims=True)

    def gather(src, dst, me, size, order, partner, ss, rr):
        copies = []
        for k in order:
            device, place = partner(k)
            copy = pltpu.make_async_remote_copy(
                src_ref=src, dst_ref=dst.at[me], send_sem=ss.at[k], recv_sem=rr.at[me],
                device_id=device, device_id_type=MESH,
            )
            copy.start()
            arrival = pltpu.make_async_remote_copy(
                src_ref=src, dst_ref=dst.at[place], send_sem=ss.at[k], recv_sem=rr.at[place],
                device_id=device, device_id_type=MESH,
            )
            copies.append((copy, arrival))
        dst[me] = src[...]
        for copy, arrival in copies:
            copy.wait_send()
            arrival.wait_recv()
        parts = [dst[k] for k in range(size)]
        while len(parts) > 1:
            parts = [parts[k] + parts[k + 1] for k in range(0, len(parts) - 1, 2)] + parts[len(parts) - len(parts) % 2 :]
        return parts[0]

    sb[...] = gather(sa, ra, me_a, size_a, far_a, partner_a, sas, sar)
    total = gather(sb, rb, me_b, size_b, far_b, partner_b, sbs, sbr)
    inner = [jnp.broadcast_to(total[:, k : k + 1], (1, 128)) for k in range(8)]
    c = inner[:2] + [2.0 * inner[k] - inner[k % 2] for k in range(2, 8)]

    def gram(i, j):
        return 0.5 * (c[i + j] + c[abs(i - j)])

    def ratio(top, bottom):
        good = jnp.logical_and(bottom > 0.0, top > 0.0)
        return jnp.where(good, top / jnp.where(good, bottom, 1.0), 0.0)

    zero = jnp.zeros_like(c[0])
    resid = [jnp.ones_like(zero)]
    direction = list(resid)
    pressure = [zero] * ITERS
    product = c[0]
    for k in range(ITERS):
        image = list(direction) + [zero]
        for j, value in enumerate(direction):
            if j == 0:
                image[1] = image[1] - value
            else:
                image[j + 1] = image[j + 1] - 0.5 * value
                image[j - 1] = image[j - 1] - 0.5 * value
        bottom = zero
        for i, value in enumerate(direction):
            line = zero
            for j, other in enumerate(image):
                line = line + other * gram(i, j)
            bottom = bottom + value * line
        alpha = ratio(product, bottom)
        for j, value in enumerate(direction):
            pressure[j] = pressure[j] + alpha * value
        if k + 1 < ITERS:
            resid = [a - alpha * b for a, b in zip(resid + [zero], image)]
            following = zero
            for i, value in enumerate(resid):
                line = zero
                for j, other in enumerate(resid):
                    line = line + other * gram(i, j)
                following = following + value * line
            beta = ratio(following, product)
            direction = [a + beta * b for a, b in zip(resid, direction + [zero])]
            product = following

    field = []
    for k in range(3):
        value = pressure[0] * basis[0][k]
        for j in range(1, ITERS):
            value = value + pressure[j] * basis[j][k]
        field.append(value)
    field_e = to_east(field)
    wet = [jnp.where(surface[k], 1.0, 0.0) for k in range(3)]
    wet_e = to_east(wet)
    for h in range(2):
        slope_e = wet[h] * wet_e[h] * (field_e[h] - field[h])
        slope_n = wet[h] * to_north(wet[h]) * (to_north(field[h]) - field[h])
        grad[0, :, 128 * h : 128 * h + 128] = slope_e[0:16]
        grad[1, :, 128 * h : 128 * h + 128] = slope_n[0:16]


def body(lats, lons, tracers, east_velocity, north_velocity, column_levels, surface_term):
    tall = 2 * LEVELS * ROWS
    cells = tracers.reshape(2 * LEVELS, ROWS, 256)
    east = east_velocity.reshape(LEVELS * ROWS, 256)
    north = north_velocity.reshape(LEVELS * ROWS, 256)
    size_a, size_b = lats // NZ, NZ * lons
    vmem = pltpu.VMEM
    scratch = [
        vmem((2, 2, LEVELS * ROWS, 128), BF16),
        vmem((2, 2, LEVELS * ROWS, 128), F32),
        vmem((ROWS, 256), jnp.int32),
        vmem((ROWS, 256), F32),
        vmem((HIGH, 2, 80, 128), F32),
        vmem((HIGH, 2, 80, 128), F32),
        vmem((HIGH, 2, 64, 128), F32),
        vmem((HIGH, 2, 64, 128), F32),
        vmem((2, 2, 64, 128), F32),
        vmem((HIGH, 2, 2, LEVELS, 128), F32),
        vmem((ROWS, 2, 64, 128), F32),
        vmem((HIGH, 8, 128), F32),
        vmem((HIGH, 8, 128), F32),
        vmem((HIGH, 8, 128), F32),
        vmem((HIGH, 8, 128), F32),
        vmem((ROWS, 8, 128), F32),
        vmem((ROWS, 8, 128), F32),
        vmem((2, 10, 8, 128), F32),
        vmem((2, 9, 8, 128), F32),
        vmem((4, 3, 8, 128), F32),
        vmem((2, 3, 2, 64, 128), BF16),
        vmem((2, 3, 2, 64, 128), BF16),
        vmem((3, 2, 2, LEVELS, 128), BF16),
        vmem((2, 2, 2, LEVELS, 128), BF16),
        vmem((3, 2, 2, LEVELS, 128), BF16),
        vmem((2, 2, 2, LEVELS, 128), BF16),
        vmem((2, 2, 2, 8, 128), F32),
        vmem((2, 2, 8, 128), F32),
        vmem((2, 2, 8, 128), F32),
        vmem((2, 2, 8, 128), F32),
        vmem((2, 8, 128), F32),
        vmem((2, 8, 128), F32),
        vmem((2, 8, 128), F32),
        vmem((2, 8, 128), F32),
        vmem((4, 8, 128), F32),
        vmem((2, 3, HIGH, 128), F32),
        vmem((ROWS, 2, 8, 128), F32),
        vmem((2, tall, 128), F32),
        vmem((1, 128), F32),
        vmem((size_a, 1, 128), F32),
        vmem((1, 128), F32),
        vmem((size_b, 1, 128), F32),
        pltpu.SemaphoreType.DMA((6 + 2 * ROWS,)),
        pltpu.SemaphoreType.DMA((15,)),
        pltpu.SemaphoreType.DMA((15,)),
        pltpu.SemaphoreType.DMA((8,)),
        pltpu.SemaphoreType.DMA((8,)),
        pltpu.SemaphoreType.DMA((size_a,)),
        pltpu.SemaphoreType.DMA((size_a,)),
        pltpu.SemaphoreType.DMA((size_b,)),
        pltpu.SemaphoreType.DMA((size_b,)),
    ]
    hbm, near = pl.BlockSpec(memory_space=pltpu.HBM), pl.BlockSpec(memory_space=pltpu.VMEM)
    updated, gradient = pl.pallas_call(
        functools.partial(kernel, lats, lons),
        out_shape=(pltpu.VMEM((tall, 256), F32), pltpu.VMEM((2, ROWS, 256), F32)),
        in_specs=[hbm] * 5,
        out_specs=(near, near),
        scratch_shapes=scratch,
        compiler_params=pltpu.CompilerParams(
            collective_id=0, has_side_effects=True, vmem_limit_bytes=40 * 1024 * 1024
        ),
    )(*[pltpu.with_memory_space_constraint(x, pltpu.HBM) for x in (cells, east, north, column_levels, surface_term)])
    return updated.reshape(2, LEVELS, ROWS, 256), gradient


def solution(mesh):
    in_specs = (
        P(None, None, "lat", "lon"),
        P(None, "lat", "lon"),
        P(None, "lat", "lon"),
        P("lat", "lon"),
        P("lat", "lon"),
    )
    out_specs = (P(None, None, "lat", "lon"), P(None, "lat", "lon"))
    step = functools.partial(body, mesh.shape["lat"], mesh.shape["lon"])
    return jax.shard_map(step, mesh=mesh, in_specs=in_specs, out_specs=out_specs, check_vma=False)
```
